256 devices in a mesh: inline: 32 (over x, z), xline: 8 (over y, core).
Axes of the slice: x: 4, y: 4, z: 8, core: 2. Of those that a mesh axis runs over, the one named last changes fastest.
Arguments:
- traces: bfloat16 [131072, 1024], P(('inline', 'xline')), may hold values from -6 to 6
- destination: int32 [131072, 1], P(('inline', 'xline')), may hold values from 0 to 255; in each aligned block of 512 rows (0 to 511, 512 to 1023, ...) at most 6 rows name the same one
- bin_local: int32 [131072], P(('inline', 'xline')), may hold values from 0 to 63
- offset_class: int32 [131072], P(('inline', 'xline')), may hold values from 0 to 7
- dip_inline: int32 [128, 128], P('inline', 'xline'), may hold values from -3 to 3
- dip_xline: int32 [128, 128], P('inline', 'xline'), may hold values from -3 to 3
Outputs:
- smoothed: float32 [8, 128, 128, 1024], P(None, 'inline', 'xline')
The draws below stay inside these ranges and needn't reach their ends.
Inputs may be any that keep to these rules, and one draw needn't show every extreme that they name: Among the traces of one device no destination occurs more than 6 times, and some destination occurs exactly 6 times.
All inputs are finite; a program needn't handle non-finite values.
Results may differ from the reference program's by a relative error of at most 0.0003.
Values may be sent and summed in bfloat16 or wider, within the bound.
A program may use at most 64 MiB of HBM per device.

```python
import math
import jax
import jax.numpy as jnp
import numpy as np
from jax import lax

SAMPLES = 1024
OFFSETS = 8
IL_TILE = 4
XL_TILE = 16
TR_DEV = 512
CAP = 6
TRACES = 131072
IL = 128
XL = 128
BIN_TILE = 64
N_XLINE = 8
DEVICES = 256


def with_ends(values, rng, smallest, largest):
    index_at = [jax.random.randint(jax.random.fold_in(rng, axis), (), 0, length) for axis, length in enumerate(values.shape)]
    longest = values.shape.index(max(values.shape))
    next_to = index_at[:longest] + [(index_at[longest] + 1) % values.shape[longest]] + index_at[longest + 1:]
    return values.at[tuple(index_at)].set(smallest).at[tuple(next_to)].set(largest)


def level_of(stream_key, shape, shards, least, top_value):
    def one(dim, blocks):
        steps = jax.random.uniform(jax.random.fold_in(jax.random.fold_in(stream_key, 6), dim), (blocks,), jnp.float32, least / len(shards), top_value / len(shards))
        return jnp.repeat(jnp.exp(steps), shape[dim] // blocks).reshape((-1,) + (1,) * (len(shape) - dim - 1))

    gain = one(*shards[0])
    for cut in shards[1:]:
        gain = gain * one(*cut)
    return gain


def assign_block(stream_key, own, number, rows, count, top, limit, skew):
    ranking = jax.random.permutation(stream_key, count)
    heavy_load, common = portions_of(count, rows * top, limit, skew, True), portions_of(count, rows * top, limit, skew, False)
    places = jnp.arange(count)

    def named(lengths, offset_by):
        used = int((lengths > 0).sum())
        fixed = max(1, used // 4)
        moved = fixed + (places - fixed + offset_by * (used - fixed)) % max(1, count - fixed)
        return jnp.zeros((count,), jnp.int32).at[ranking[jnp.where(places < fixed, places, moved)]].set(jnp.asarray(lengths, jnp.int32))

    lengths = jnp.where(number % 4 == 0, named(heavy_load, number // 4), named(common, number - number // 4 - 1))
    mixed = jax.random.permutation(jax.random.fold_in(own, 3), count)
    donor, receiver = mixed[0:count // 2 * 2:2], mixed[1:count // 2 * 2:2]
    slack = jnp.minimum(lengths[donor] - 1, limit - lengths[receiver]) // 2
    slack = jnp.where((donor == ranking[0]) | (receiver == ranking[0]) | (lengths[receiver] == 0), 0, jnp.maximum(slack, 0))
    moved = jax.random.randint(jax.random.fold_in(own, 4), (count // 2,), 0, 1 << 20) % (slack + 1)
    lengths = lengths.at[donor].add(-moved).at[receiver].add(moved)
    labels = jnp.searchsorted(jnp.cumsum(lengths), jnp.arange(rows * top), side="right").astype(jnp.int32)
    grid = labels.reshape(top, rows).T
    grid = grid[jax.random.permutation(jax.random.fold_in(own, 1), rows)]
    offset_by = jax.random.randint(jax.random.fold_in(own, 2), (rows, 1), 0, top)
    return jnp.take_along_axis(grid, (jnp.arange(top)[None, :] + offset_by) % top, axis=1)


def portions_of(number_of, total, limit, slope, full):
    weights = [(1 << 20) // math.isqrt(grade ** slope) + 1 for grade in range(1, number_of + 1)]
    largest = limit if full else min(limit, max(-(-total // number_of), total * weights[0] // sum(weights)))
    least = 1 if total - largest >= number_of - 1 else 0
    given, spare = [largest] + [least] * (number_of - 1), total - largest - least * (number_of - 1)
    while spare > 0:
        movable = [i for i in range(1, number_of) if given[i] < largest] or [i for i in range(1, number_of) if given[i] < limit]
        whole, left = sum([weights[i] for i in movable]), spare
        for i in movable:
            addition = min(limit - given[i], max(1, left * weights[i] // whole), spare)
            given[i] = given[i] + addition
            spare = spare - addition
    return np.array(given)


def normal_values(rng, dims, spread, bound, split=(), kind=jnp.bfloat16):
    result = spread * jax.random.normal(rng, dims, jnp.float32)
    if split:
        result = result * level_of(rng, dims, split, -0.22, 0.18)
    return jnp.clip(result, -bound, bound).astype(kind)


def setup_inputs(seed: int = 0) -> dict:
    seeds = jax.random.split(jax.random.key(seed), 7)
    traces = normal_values(seeds[0], (TRACES, SAMPLES), 1.0, 6.0, ((0, 256),))
    destination_keys = jax.random.split(jax.random.fold_in(seeds[1], 1), TRACES // TR_DEV)
    destination_turns = jax.random.permutation(jax.random.fold_in(seeds[1], 3), TRACES // TR_DEV)
    destination = jax.vmap(lambda own, number: assign_block(jax.random.fold_in(seeds[1], 2), own, number, TR_DEV, DEVICES, 1, CAP, 2))(destination_keys, destination_turns).reshape((TRACES, 1))
    bin_local = with_ends(jax.random.randint(seeds[2], (TRACES,), 0, BIN_TILE), jax.random.fold_in(seeds[2], 1), 0, BIN_TILE - 1).astype(jnp.int32)
    offset_class = with_ends(jax.random.randint(seeds[3], (TRACES,), 0, OFFSETS), jax.random.fold_in(seeds[3], 1), 0, OFFSETS - 1).astype(jnp.int32)
    dip_inline = with_ends(jax.random.randint(seeds[4], (IL, XL), -3, 4), jax.random.fold_in(seeds[4], 1), -3, 3).astype(jnp.int32)
    dip_xline = with_ends(jax.random.randint(seeds[5], (IL, XL), -3, 4), jax.random.fold_in(seeds[5], 1), -3, 3).astype(jnp.int32)
    return {"traces": traces, "destination": destination, "bin_local": bin_local, "offset_class": offset_class, "dip_inline": dip_inline, "dip_xline": dip_xline}


FILTER_TAPS = (0.05, 0.08, 0.12, 0.15, 0.2, 0.15, 0.12, 0.08, 0.05)
dip_limit = 3
time_pad = 12


def dip_pass(padded, dips, axis, count, samples):
    running = None
    for tap_index in range(9):
        neighbour = lax.slice_in_dim(padded, tap_index, tap_index + count, axis=axis)
        shifted = jnp.zeros(neighbour.shape[:-1] + (samples,), jnp.float32)
        for dip_value in range(-dip_limit, dip_limit + 1):
            first_sample = time_pad + (tap_index - 4) * dip_value
            shifted = jnp.where((dips == dip_value)[..., None], neighbour[..., first_sample:first_sample + samples], shifted)
        term = FILTER_TAPS[tap_index] * shifted
        running = term if running is None else running + term
    return running


def reference(traces, destination, bin_local, offset_class, dip_inline, dip_xline):
    target = destination[:, 0]
    tile_inline = target // N_XLINE
    tile_xline = target % N_XLINE
    row_index = tile_inline * IL_TILE + bin_local // XL_TILE
    column_index = tile_xline * XL_TILE + bin_local % XL_TILE
    cell_index = (row_index * XL + column_index).astype(jnp.int32)
    values = traces.astype(jnp.float32)

    def one_class(class_index):
        segment_ids = jnp.where(offset_class == class_index, cell_index, IL * XL).astype(jnp.int32)
        totals = jax.ops.segment_sum(values, segment_ids, IL * XL + 1)[:IL * XL]
        counts = jax.ops.segment_sum(jnp.ones(segment_ids.shape, jnp.float32), segment_ids, IL * XL + 1)[:IL * XL]
        stacked = (totals / jnp.maximum(counts, 1.0)[:, None]).reshape(IL, XL, SAMPLES)
        padded = jnp.pad(stacked, ((4, 4), (0, 0), (time_pad, time_pad)))
        smoothed = dip_pass(padded, dip_inline, 0, IL, SAMPLES)
        padded = jnp.pad(smoothed, ((0, 0), (4, 4), (time_pad, time_pad)))
        return dip_pass(padded, dip_xline, 1, XL, SAMPLES)

    return lax.map(one_class, jnp.arange(OFFSETS, dtype=jnp.int32))
```

```python
import jax
import jax.numpy as jnp
from jax import lax
from jax.experimental import pallas as pl
from jax.experimental.pallas import tpu as pltpu
from jax.sharding import PartitionSpec as P

OFFSETS = 8
FILTER_TAPS = (0.05, 0.08, 0.12, 0.15, 0.2, 0.15, 0.12, 0.08, 0.05)
dip_limit = 3
time_pad = 12

MESH = pl.DeviceIdType.MESH
N_Z = 8
N_P = 32
N_XL = 8
CAP = 6
POOL = 96
SLOTS = N_Z * CAP
ROWS = N_P * SLOTS
CELLS = 512
T = 4
NT = (((1,), (1,)), ((), ()))
f32, bf16, i32 = jnp.float32, jnp.bfloat16, jnp.int32


def iota(shape, dim):
    return lax.broadcasted_iota(i32, shape, dim)


def onehot(mask):
    return jnp.where(mask, 1.0, 0.0).astype(bf16)


def route_kernel(
    traces, dest, bins, offs, stacked, flag_out,
    rows, p1, send1, recv1, lab1s, lab1r, l2, p2, send2, recv2, lab2s, lab2r, wide, sel, count,
    s1_send, s1_recv, l1_send, l1_recv, s2_send, s2_recv, l2_send, l2_recv,
):
    n, samples = traces.shape
    w = samples // T
    me_i = lax.axis_index("inline")
    me_x = lax.axis_index("xline")
    my_z = lax.rem(me_i, N_Z)
    my_col = me_i // N_Z
    my_p = my_col * N_XL + me_x

    def z_peer(k):
        z = lax.rem(my_z + k, N_Z)
        return z, (my_col * N_Z + z, me_x)

    def p_peer(k):
        p = lax.rem(my_p + k, N_P)
        return p, ((p // N_XL) * N_Z + my_z, lax.rem(p, N_XL))

    barrier = pltpu.get_barrier_semaphore()

    @pl.loop(1, N_Z)
    def _(k):
        pl.semaphore_signal(barrier, inc=1, device_id=z_peer(k)[1], device_id_type=MESH)

    @pl.loop(1, N_P)
    def _(k):
        pl.semaphore_signal(barrier, inc=1, device_id=p_peer(k)[1], device_id_type=MESH)

    d = dest[...]
    eye = onehot(iota((n, n), 0) == iota((n, n), 1))
    wide_d = jnp.broadcast_to(d.astype(f32), (128, n)).astype(bf16)
    dcol = lax.dot_general(eye, wide_d, NT, preferred_element_type=f32).astype(i32)
    zcol = (dcol >> 3) & 7
    for t in range(n // 128):
        lanes = slice(t * 128, (t + 1) * 128)
        drow = d[:, lanes]
        earlier = iota((n, 128), 0) < iota((n, 128), 1) + t * 128
        same = (dcol == drow) & earlier
        same_z = (zcol == ((drow >> 3) & 7)) & earlier
        rows[0:1, lanes] = jnp.sum(jnp.where(same, 1.0, 0.0), axis=0, keepdims=True)
        rows[1:2, lanes] = jnp.sum(jnp.where(same_z, 1.0, 0.0), axis=0, keepdims=True)
    position = rows[0:1, :].astype(i32)
    place = rows[1:2, :].astype(i32)
    zrow = (d >> 3) & 7
    plane = (d >> 6) * N_XL + (d & 7)
    over = jnp.max(place, axis=1, keepdims=True) >= POOL
    over = jnp.where(over, 1, 0)
    sub = iota((16, n), 0)
    labels = jnp.where(sub == 0, plane, 0)
    labels = jnp.where(sub == 1, my_z * CAP + position + 1, labels)
    labels = jnp.where(sub == 2, bins[...], labels)
    labels = jnp.where(sub == 3, offs[...], labels)
    labels = labels.astype(f32).astype(bf16)

    @pl.loop(0, N_Z)
    def _(z):
        target = jnp.where(zrow == z, place, -1)
        pick = onehot(iota((128, n), 0) == target)
        p1[z] = pick
        lab = lax.dot_general(labels, pick, NT, preferred_element_type=f32)[:8].astype(i32)
        lab = jnp.where(iota((8, 128), 1) < POOL, lab, 0)
        lab1s[z] = jnp.where(iota((8, 128), 0) == 4, over, lab)

    lab1r[my_z] = lab1s[my_z]

    @pl.loop(0, T * N_Z)
    def _(i):
        recv1[i // N_Z, lax.rem(i, N_Z), POOL:, :] = jnp.zeros((128 - POOL, w), bf16)

    pl.semaphore_wait(barrier, N_Z - 1 + N_P - 1)

    def lab1_copy(k):
        z, peer = z_peer(k)
        return pltpu.make_async_remote_copy(
            src_ref=lab1s.at[z], dst_ref=lab1r.at[my_z],
            send_sem=l1_send.at[k], recv_sem=l1_recv.at[k],
            device_id=peer, device_id_type=MESH,
        )

    def row1_copy(t, k):
        z, peer = z_peer(k)
        return pltpu.make_async_remote_copy(
            src_ref=send1.at[t, z], dst_ref=recv1.at[t, my_z, pl.ds(0, POOL), :],
            send_sem=s1_send.at[t, k], recv_sem=s1_recv.at[t, k],
            device_id=peer, device_id_type=MESH,
        )

    def lab2_copy(k):
        p, peer = p_peer(k)
        return pltpu.make_async_remote_copy(
            src_ref=lab2s.at[p], dst_ref=lab2r.at[my_p],
            send_sem=l2_send.at[k], recv_sem=l2_recv.at[k],
            device_id=peer, device_id_type=MESH,
        )

    def row2_copy(t, k):
        p, peer = p_peer(k)
        return pltpu.make_async_remote_copy(
            src_ref=send2.at[t, p], dst_ref=recv2.at[t, my_p],
            send_sem=s2_send.at[t, k], recv_sem=s2_recv.at[t, k],
            device_id=peer, device_id_type=MESH,
        )

    @pl.loop(1, N_Z)
    def _(k):
        lab1_copy(k).start()

    for t in range(T):
        cols = slice(t * w, (t + 1) * w)

        def picked(z, cols=cols):
            return jnp.dot(p1[z][:POOL], traces[:, cols], preferred_element_type=f32).astype(bf16)

        @pl.loop(1, N_Z)
        def _(k, t=t, picked=picked):
            z, _peer = z_peer(k)
            send1[t, z] = picked(z)
            row1_copy(t, k).start()

        recv1[t, my_z, 0:POOL, :] = picked(my_z)

    @pl.loop(1, N_Z)
    def _(k):
        lab1_copy(k).wait()

    def seen(z, worst):
        lab = lab1r[z]
        code = lab[1:2, :]
        target = jnp.where(code > 0, lab[0:1, :] * SLOTS + code - 1, -1)
        lanes = pl.ds(pl.multiple_of(z * 128, 128), 128)
        p2[:, lanes] = onehot(iota((ROWS, 128), 0) == target)
        l2[:, lanes] = jnp.concatenate([lab, lab], axis=0).astype(f32).astype(bf16)
        return jnp.maximum(worst, lab[4:5, :])

    worst = lax.fori_loop(0, N_Z, seen, jnp.zeros((1, 128), i32))
    lab = lax.dot_general(l2[...], p2[...], NT, preferred_element_type=f32).astype(i32)
    cell = jnp.where(lab[1:2, :] > 0, lab[2:3, :] * OFFSETS + lab[3:4, :], -1)
    wide[...] = jnp.where(iota((8, ROWS), 0) == 1, worst[:, 0:1], cell)

    @pl.loop(0, N_P // 8)
    def _(g):
        part = wide[:, pl.ds(pl.multiple_of(g * 8 * SLOTS, 128), 8 * SLOTS)]
        for i in range(8):
            lab2s[g * 8 + i, :, 0:SLOTS] = part[:, i * SLOTS:(i + 1) * SLOTS]

    lab2r[my_p] = lab2s[my_p]

    @pl.loop(1, N_P)
    def _(k):
        lab2_copy(k).start()

    def forward(t):
        @pl.loop(1, N_Z)
        def _(k):
            row1_copy(t, k).wait()

        arrived = recv1[t].reshape(N_Z * 128, w)

        @pl.loop(0, N_P // 8)
        def _(g):
            pick = p2[pl.ds(pl.multiple_of(g * 8 * SLOTS, 128), 8 * SLOTS), :]
            out = jnp.dot(pick, arrived, preferred_element_type=f32).astype(bf16)
            send2[t, pl.ds(g * 8, 8)] = out.reshape(8, SLOTS, w)

        @pl.loop(1, N_P)
        def _(k):
            row2_copy(t, k).start()

        recv2[t, my_p] = send2[t, my_p]

    def selector():
        @pl.loop(1, N_P)
        def _(k):
            lab2_copy(k).wait()

        @pl.loop(0, N_P // 8)
        def _(g):
            part = jnp.concatenate([lab2r[g * 8 + i][:, 0:SLOTS] for i in range(8)], axis=1)
            wide[:, pl.ds(pl.multiple_of(g * 8 * SLOTS, 128), 8 * SLOTS)] = part

        @pl.loop(0, ROWS // 128)
        def _(c):
            lanes = pl.ds(pl.multiple_of(c * 128, 128), 128)
            sel[:, lanes] = onehot(iota((CELLS, 128), 0) == wide[0:1, lanes])

        traces_per_cell = jnp.dot(sel[...], jnp.ones((ROWS, 128), bf16), preferred_element_type=f32)
        count[...] = jnp.maximum(traces_per_cell, 1.0)
        flag_out[...] = jnp.broadcast_to(jnp.max(wide[1:2, :], axis=1, keepdims=True), (8, 128))

    def stack(t):
        @pl.loop(1, N_P)
        def _(k):
            row2_copy(t, k).wait()

        total = jnp.dot(sel[...], recv2[t].reshape(ROWS, w), preferred_element_type=f32)
        for c in range(w // 128):
            stacked[:, t * w + c * 128:t * w + (c + 1) * 128] = total[:, c * 128:(c + 1) * 128] / count[...]

    for t in range(T):
        forward(t)
        if t == 0:
            selector()
        if t > 0:
            stack(t - 1)
    stack(T - 1)


def route(traces, dest, bins, offs):
    n, samples = traces.shape
    w = samples // T
    vmem = pl.BlockSpec(memory_space=pltpu.VMEM)
    dma = pltpu.SemaphoreType.DMA
    return pl.pallas_call(
        route_kernel,
        out_shape=(
            jax.ShapeDtypeStruct((CELLS, samples), f32),
            jax.ShapeDtypeStruct((8, 128), i32),
        ),
        in_specs=[vmem] * 4,
        out_specs=(vmem, vmem),
        scratch_shapes=[
            pltpu.VMEM((8, n), f32),
            pltpu.VMEM((N_Z, 128, n), bf16),
            pltpu.VMEM((T, N_Z, POOL, w), bf16),
            pltpu.VMEM((T, N_Z, 128, w), bf16),
            pltpu.VMEM((N_Z, 8, 128), i32),
            pltpu.VMEM((N_Z, 8, 128), i32),
            pltpu.VMEM((16, N_Z * 128), bf16),
            pltpu.VMEM((ROWS, N_Z * 128), bf16),
            pltpu.VMEM((T, N_P, SLOTS, w), bf16),
            pltpu.VMEM((T, N_P, SLOTS, w), bf16),
            pltpu.VMEM((N_P, 8, 128), i32),
            pltpu.VMEM((N_P, 8, 128), i32),
            pltpu.VMEM((8, ROWS), i32),
            pltpu.VMEM((CELLS, ROWS), bf16),
            pltpu.VMEM((CELLS, 128), f32),
            dma((T, N_Z)), dma((T, N_Z)), dma((N_Z,)), dma((N_Z,)),
            dma((T, N_P)), dma((T, N_P)), dma((N_P,)), dma((N_P,)),
        ],
        compiler_params=pltpu.CompilerParams(
            collective_id=0, has_side_effects=True, vmem_limit_bytes=48 * 1024 * 1024
        ),
    )(traces, dest, bins, offs)


def steer(blocks, dip):
    samples = blocks(0).shape[1]
    parts = samples // 128
    lane = iota((8, 128), 1)

    def signed(up):
        acc = [FILTER_TAPS[4] * blocks(0)[:, k * 128:(k + 1) * 128] for k in range(parts)]
        zero = jnp.zeros((8, 128), f32)
        for j in (-4, -3, -2, -1, 1, 2, 3, 4):
            shift = j * dip
            block = blocks(j)
            turn = lax.rem(128 - shift, 128)
            turned = [pltpu.roll(block[:, k * 128:(k + 1) * 128], turn, 1) for k in range(parts)]
            if up == (j > 0):
                keep = lane < 128 - shift
                other = turned[1:] + [zero]
            else:
                keep = lane >= -shift
                other = [zero] + turned[:-1]
            for k in range(parts):
                acc[k] += FILTER_TAPS[j + 4] * jnp.where(keep, turned[k], other[k])
        return acc

    return lax.cond(dip >= 0, lambda: signed(True), lambda: signed(False))


def inline_kernel(dips, before, own, after, out):
    n_il, n_xl = own.shape[0], own.shape[1]
    base = pl.program_id(0) * n_xl

    @pl.loop(0, n_xl)
    def _(x):
        for i in range(n_il):
            def blocks(j, i=i):
                at = i + j
                ref = before if at < 0 else own if at < n_il else after
                return ref[at % n_il, x]

            acc = steer(blocks, dips[i, base + x])
            for k, part in enumerate(acc):
                out[i, x, :, k * 128:(k + 1) * 128] = part


def inline_pass(dips, before, own, after):
    n_il, n_xl, _, samples = own.shape
    step = 4
    block = pl.BlockSpec((n_il, step, OFFSETS, samples), lambda s: (0, s, 0, 0))
    return pl.pallas_call(
        inline_kernel,
        grid=(n_xl // step,),
        out_shape=jax.ShapeDtypeStruct(own.shape, f32),
        in_specs=[pl.BlockSpec(memory_space=pltpu.SMEM), block, block, block],
        out_specs=block,
        compiler_params=pltpu.CompilerParams(vmem_limit_bytes=32 * 1024 * 1024),
    )(dips, before, own, after)


def xline_kernel(dips, left, own, right, out, ext, turned):
    n_xl = own.shape[1]
    il = pl.program_id(0)
    ext[0:4] = left[0]
    ext[4:4 + n_xl] = own[0]
    ext[4 + n_xl:] = right[0]

    @pl.loop(0, n_xl)
    def _(x):
        acc = steer(lambda j: ext[x + 4 + j], dips[il, x])
        for k, part in enumerate(acc):
            turned[k, pl.ds(x, OFFSETS, stride=n_xl), :] = part

    for k in range(turned.shape[0]):
        out[:, 0, :, k * 128:(k + 1) * 128] = turned[k].reshape(OFFSETS, n_xl, 128)


def xline_pass(dips, left, own, right):
    n_il, n_xl, _, samples = own.shape
    side = pl.BlockSpec((1, 4, OFFSETS, samples), lambda s: (s, 0, 0, 0))
    return pl.pallas_call(
        xline_kernel,
        grid=(n_il,),
        out_shape=jax.ShapeDtypeStruct((OFFSETS, n_il, n_xl, samples), f32),
        in_specs=[
            pl.BlockSpec(memory_space=pltpu.SMEM),
            side,
            pl.BlockSpec((1, n_xl, OFFSETS, samples), lambda s: (s, 0, 0, 0)),
            side,
        ],
        out_specs=pl.BlockSpec((OFFSETS, 1, n_xl, samples), lambda s: (0, s, 0, 0)),
        scratch_shapes=[
            pltpu.VMEM((n_xl + 8, OFFSETS, samples), f32),
            pltpu.VMEM((samples // 128, OFFSETS * n_xl, 128), f32),
        ],
        compiler_params=pltpu.CompilerParams(vmem_limit_bytes=32 * 1024 * 1024),
    )(dips, left, own, right)


def shifted(cells, axis):
    count = lax.axis_size(axis)
    return (
        lambda tail: lax.ppermute(tail, axis, [(i, i + 1) for i in range(count - 1)]),
        lambda head: lax.ppermute(head, axis, [(i + 1, i) for i in range(count - 1)]),
    )


def padded_2(cells, sides, width):
    for axis, dim in sides:
        count = lax.axis_size(axis)
        ends = count - 1
        head = lax.slice_in_dim(cells, 0, width, axis=dim)
        tail = lax.slice_in_dim(cells, cells.shape[dim] - width, cells.shape[dim], axis=dim)
        cells = jnp.concatenate(
            [
                lax.ppermute(tail, axis, [(i, (i + 1) % count) for i in range(ends)]),
                cells,
                lax.ppermute(head, axis, [((i + 1) % count, i) for i in range(ends)]),
            ],
            axis=dim,
        )
    return cells


def dip_pass(padded, dips, axis, count, samples):
    running = None
    for tap_index in range(9):
        neighbour = lax.slice_in_dim(padded, tap_index, tap_index + count, axis=axis)
        moved = jnp.zeros(neighbour.shape[:-1] + (samples,), jnp.float32)
        for dip_value in range(-dip_limit, dip_limit + 1):
            first_sample = time_pad + (tap_index - 4) * dip_value
            moved = jnp.where(
                (dips == dip_value)[..., None],
                neighbour[..., first_sample : first_sample + samples],
                moved,
            )
        term = FILTER_TAPS[tap_index] * moved
        running = term if running is None else running + term
    return running


def any_load(traces, destination, bin_local, offset_class, dip_inline, dip_xline):
    n_inline = lax.axis_size("inline")
    n_xline = lax.axis_size("xline")
    devices = n_inline * n_xline
    row_count, samples = traces.shape
    capacity = 3 * row_count // devices
    inline_bins, xline_bins = dip_inline.shape
    bin_count = inline_bins * xline_bins
    target = destination[:, 0]
    matches = (target[:, None] == jnp.arange(devices, dtype=jnp.int32)[None, :]).astype(jnp.int32)
    before = jnp.cumsum(matches, axis=0) - matches
    position = jnp.sum(before * matches, axis=1)
    slot_index = target * capacity + position
    labels = offset_class * bin_count + bin_local
    outgoing = jnp.zeros((devices * capacity, samples), jnp.bfloat16).at[slot_index].set(traces)
    outgoing = outgoing.reshape(n_inline, n_xline, capacity, samples)
    out_labels = jnp.full((devices * capacity,), -1, jnp.int32).at[slot_index].set(labels)
    out_labels = out_labels.reshape(n_inline, n_xline, capacity)

    def exchange(value):
        value = lax.all_to_all(value, "inline", split_axis=0, concat_axis=0, tiled=True)
        return lax.all_to_all(value, "xline", split_axis=1, concat_axis=1, tiled=True)

    received = exchange(outgoing).reshape(-1, samples)
    got_labels = exchange(out_labels).reshape(-1)
    cell_total = OFFSETS * bin_count
    selector = jnp.arange(cell_total, dtype=jnp.int32)[:, None] == got_labels[None, :]
    totals = jnp.dot(selector.astype(jnp.bfloat16), received, preferred_element_type=jnp.float32)
    counts = jnp.sum(selector.astype(jnp.int32), axis=1).astype(jnp.float32)
    stacked = (totals / jnp.maximum(counts, 1.0)[:, None]).reshape(
        OFFSETS, inline_bins, xline_bins, samples
    )
    with_rim = padded_2(stacked, (("inline", 1),), 4)
    padded = jnp.pad(with_rim, ((0, 0), (0, 0), (0, 0), (time_pad, time_pad)))
    smoothed = dip_pass(padded, dip_inline, 1, inline_bins, samples)
    with_rim = padded_2(smoothed, (("xline", 2),), 4)
    padded = jnp.pad(with_rim, ((0, 0), (0, 0), (0, 0), (time_pad, time_pad)))
    return dip_pass(padded, dip_xline, 2, xline_bins, samples)


def per_device(traces, destination, bin_local, offset_class, dip_inline, dip_xline):
    n, samples = traces.shape
    n_il, n_xl = dip_inline.shape
    stacked, flag = route(
        traces, destination.reshape(1, n), bin_local.reshape(1, n), offset_class.reshape(1, n)
    )
    stacked = stacked.reshape(n_il, n_xl, OFFSETS, samples)
    up, down = shifted(stacked, "inline")
    first = inline_pass(dip_inline, up(stacked), stacked, down(stacked))
    right, left = shifted(first, "xline")
    from_left = right(first[:, n_xl - 4:])
    from_right = left(first[:, :4])
    return lax.cond(
        flag[0, 0] > 0,
        lambda: any_load(traces, destination, bin_local, offset_class, dip_inline, dip_xline),
        lambda: xline_pass(dip_xline, from_left, first, from_right),
    )


def solution(mesh):
    return jax.shard_map(
        per_device,
        mesh=mesh,
        in_specs=(
            P(("inline", "xline"), None),
            P(("inline", "xline"), None),
            P(("inline", "xline")),
            P(("inline", "xline")),
            P("inline", "xline"),
            P("inline", "xline"),
        ),
        out_specs=P(None, "inline", "xline", None),
        check_vma=False,
    )
```

```python
import jax
import jax.numpy as jnp
from jax import lax
from jax.experimental import pallas as pl
from jax.experimental.pallas import tpu as pltpu
from jax.sharding import PartitionSpec as P

OFFSETS = 8
FILTER_TAPS = (0.05, 0.08, 0.12, 0.15, 0.2, 0.15, 0.12, 0.08, 0.05)
dip_limit = 3
time_pad = 12

MESH = pl.DeviceIdType.MESH
N_Z = 8
N_P = 32
N_XL = 8
N_IL = 32
CAP = 6
POOL = 96
SLOTS = N_Z * CAP
ROWS = N_P * SLOTS
CELLS = 512
T = 4
NT = (((1,), (1,)), ((), ()))
f32, bf16, i32 = jnp.float32, jnp.bfloat16, jnp.int32


def iota(shape, dim):
    return lax.broadcasted_iota(i32, shape, dim)


def onehot(mask):
    return jnp.where(mask, 1.0, 0.0).astype(bf16)


def route_kernel(
    traces, dest, bins, offs, ext, flag_out,
    rows, eye, p1, send1, recv1, lab1s, lab1r, l2, p2, send2, recv2, lab2s, lab2r, wide, sel, count,
    rim_q, rim_s, got_q, got_s,
    s1_send, s1_recv, l1_send, l1_recv, s2_send, s2_recv, l2_send, l2_recv,
    q_send, q_recv, f_send, f_recv,
):
    n, samples = traces.shape
    w = samples // T
    me_i = lax.axis_index("inline")
    me_x = lax.axis_index("xline")
    my_z = lax.rem(me_i, N_Z)
    my_col = me_i // N_Z
    my_p = my_col * N_XL + me_x

    def z_peer(k):
        z = lax.rem(my_z + k, N_Z)
        return z, (my_col * N_Z + z, me_x)

    def p_peer(k):
        p = lax.rem(my_p + k, N_P)
        return p, ((p // N_XL) * N_Z + my_z, lax.rem(p, N_XL))

    def rim_peer(side):
        return (lax.rem(me_i + (1 if side == 0 else N_IL - 1), N_IL), me_x)

    barrier = pltpu.get_barrier_semaphore()
    for side in range(2):
        pl.semaphore_signal(barrier, inc=1, device_id=rim_peer(side), device_id_type=MESH)

    @pl.loop(1, N_Z)
    def _(k):
        pl.semaphore_signal(barrier, inc=1, device_id=z_peer(k)[1], device_id_type=MESH)

    @pl.loop(1, N_P)
    def _(k):
        pl.semaphore_signal(barrier, inc=1, device_id=p_peer(k)[1], device_id_type=MESH)

    d = dest[...]
    eye[...] = onehot(iota((n, n), 0) == iota((n, n), 1))
    wide_d = jnp.broadcast_to(d.astype(f32), (128, n)).astype(bf16)
    dcol = lax.dot_general(eye[...], wide_d, NT, preferred_element_type=f32).astype(i32)
    zcol = (dcol >> 3) & 7
    for t in range(n // 128):
        lanes = slice(t * 128, (t + 1) * 128)
        drow = d[:, lanes]
        earlier = iota((n, 128), 0) < iota((n, 128), 1) + t * 128
        same = (dcol == drow) & earlier
        same_z = (zcol == ((drow >> 3) & 7)) & earlier
        rows[0:1, lanes] = jnp.sum(jnp.where(same, 1.0, 0.0), axis=0, keepdims=True)
        rows[1:2, lanes] = jnp.sum(jnp.where(same_z, 1.0, 0.0), axis=0, keepdims=True)
    position = rows[0:1, :].astype(i32)
    place = rows[1:2, :].astype(i32)
    zrow = (d >> 3) & 7
    plane = (d >> 6) * N_XL + (d & 7)
    over = jnp.max(place, axis=1, keepdims=True) >= POOL
    over = jnp.where(over, 1, 0)
    sub = iota((16, n), 0)
    labels = jnp.where(sub == 0, plane, 0)
    labels = jnp.where(sub == 1, my_z * CAP + position + 1, labels)
    labels = jnp.where(sub == 2, bins[...], labels)
    labels = jnp.where(sub == 3, offs[...], labels)
    labels = labels.astype(f32).astype(bf16)

    @pl.loop(0, N_Z)
    def _(z):
        target = jnp.where(zrow == z, place, -1)
        pick = onehot(iota((128, n), 0) == target)
        p1[z] = pick
        lab = lax.dot_general(labels, pick, NT, preferred_element_type=f32)[:8].astype(i32)
        lab = jnp.where(iota((8, 128), 1) < POOL, lab, 0)
        lab1s[z] = jnp.where(iota((8, 128), 0) == 4, over, lab)

    lab1r[my_z] = lab1s[my_z]

    @pl.loop(0, T * N_Z)
    def _(i):
        recv1[i // N_Z, lax.rem(i, N_Z), POOL:, :] = jnp.zeros((128 - POOL, w), bf16)

    pl.semaphore_wait(barrier, N_Z - 1 + N_P - 1 + 2)

    def lab1_copy(k):
        z, peer = z_peer(k)
        return pltpu.make_async_remote_copy(
            src_ref=lab1s.at[z], dst_ref=lab1r.at[my_z],
            send_sem=l1_send.at[k], recv_sem=l1_recv.at[k],
            device_id=peer, device_id_type=MESH,
        )

    def row1_copy(t, k):
        z, peer = z_peer(k)
        return pltpu.make_async_remote_copy(
            src_ref=send1.at[t, z], dst_ref=recv1.at[t, my_z, pl.ds(0, POOL), :],
            send_sem=s1_send.at[t, k], recv_sem=s1_recv.at[t, k],
            device_id=peer, device_id_type=MESH,
        )

    def lab2_copy(k):
        p, peer = p_peer(k)
        return pltpu.make_async_remote_copy(
            src_ref=lab2s.at[p], dst_ref=lab2r.at[my_p],
            send_sem=l2_send.at[k], recv_sem=l2_recv.at[k],
            device_id=peer, device_id_type=MESH,
        )

    def row2_copy(t, k):
        p, peer = p_peer(k)
        return pltpu.make_async_remote_copy(
            src_ref=send2.at[t, p], dst_ref=recv2.at[t, my_p],
            send_sem=s2_send.at[t, k], recv_sem=s2_recv.at[t, k],
            device_id=peer, device_id_type=MESH,
        )

    @pl.loop(1, N_Z)
    def _(k):
        lab1_copy(k).start()

    for t in range(T):
        cols = slice(t * w, (t + 1) * w)

        def picked(z, cols=cols):
            return jnp.dot(p1[z][:POOL], traces[:, cols], preferred_element_type=f32).astype(bf16)

        @pl.loop(1, N_Z)
        def _(k, t=t, picked=picked):
            z, _peer = z_peer(k)
            send1[t, z] = picked(z)
            row1_copy(t, k).start()

        recv1[t, my_z, 0:POOL, :] = picked(my_z)

    @pl.loop(1, N_Z)
    def _(k):
        lab1_copy(k).wait()

    def seen(z, worst):
        lab = lab1r[z]
        code = lab[1:2, :]
        target = jnp.where(code > 0, lab[0:1, :] * SLOTS + code - 1, -1)
        lanes = pl.ds(pl.multiple_of(z * 128, 128), 128)
        p2[:, lanes] = onehot(iota((ROWS, 128), 0) == target)
        l2[:, lanes] = jnp.concatenate([lab, lab], axis=0).astype(f32).astype(bf16)
        return jnp.maximum(worst, lab[4:5, :])

    worst = lax.fori_loop(0, N_Z, seen, jnp.zeros((1, 128), i32))
    lab = lax.dot_general(l2[...], p2[...], NT, preferred_element_type=f32).astype(i32)
    cell = jnp.where(lab[1:2, :] > 0, lab[2:3, :] * OFFSETS + lab[3:4, :], -1)
    wide[...] = jnp.where(iota((8, ROWS), 0) == 1, worst[:, 0:1], cell)

    @pl.loop(0, N_P // 8)
    def _(g):
        part = wide[:, pl.ds(pl.multiple_of(g * 8 * SLOTS, 128), 8 * SLOTS)]
        for i in range(8):
            lab2s[g * 8 + i, :, 0:SLOTS] = part[:, i * SLOTS:(i + 1) * SLOTS]

    lab2r[my_p] = lab2s[my_p]

    @pl.loop(1, N_P)
    def _(k):
        lab2_copy(k).start()

    def forward(t):
        @pl.loop(1, N_Z)
        def _(k):
            row1_copy(t, k).wait()

        arrived = recv1[t].reshape(N_Z * 128, w)

        @pl.loop(0, N_P // 8)
        def _(g):
            pick = p2[pl.ds(pl.multiple_of(g * 8 * SLOTS, 128), 8 * SLOTS), :]
            out = jnp.dot(pick, arrived, preferred_element_type=f32).astype(bf16)
            send2[t, pl.ds(g * 8, 8)] = out.reshape(8, SLOTS, w)

        @pl.loop(1, N_P)
        def _(k):
            row2_copy(t, k).start()

        recv2[t, my_p] = send2[t, my_p]

    def selector():
        @pl.loop(1, N_P)
        def _(k):
            lab2_copy(k).wait()

        @pl.loop(0, N_P // 8)
        def _(g):
            part = jnp.concatenate([lab2r[g * 8 + i][:, 0:SLOTS] for i in range(8)], axis=1)
            wide[:, pl.ds(pl.multiple_of(g * 8 * SLOTS, 128), 8 * SLOTS)] = part

        @pl.loop(0, ROWS // 128)
        def _(c):
            lanes = pl.ds(pl.multiple_of(c * 128, 128), 128)
            sel[:, lanes] = onehot(iota((CELLS, 128), 0) == wide[0:1, lanes])

        traces_per_cell = jnp.dot(sel[...], jnp.ones((ROWS, 128), bf16), preferred_element_type=f32)
        count[...] = jnp.maximum(traces_per_cell, 1.0)
        flag_out[...] = jnp.broadcast_to(jnp.max(wide[1:2, :], axis=1, keepdims=True), (8, 128))

    def stack(t):
        @pl.loop(1, N_P)
        def _(k):
            row2_copy(t, k).wait()

        total = jnp.dot(sel[...], recv2[t].reshape(ROWS, w), preferred_element_type=f32)
        parts = [total[:, c * 128:(c + 1) * 128] / count[...] for c in range(w // 128)]
        top = jnp.abs(parts[0])
        for c, part in enumerate(parts):
            ext[CELLS:2 * CELLS, t * w + c * 128:t * w + (c + 1) * 128] = part
            top = jnp.maximum(top, jnp.abs(part))
        step = (jnp.max(top, axis=1, keepdims=True) * (1.01 / 32767.0)).astype(bf16)
        step = jnp.broadcast_to(step, (CELLS, 128))
        size = step.astype(f32)
        fine = jnp.where(size > 0.0, 1.0 / size, 0.0)
        for c, part in enumerate(parts):
            rim_q[t, :, c * 128:(c + 1) * 128] = jnp.round(part * fine).astype(i32).astype(jnp.int16)
        first_lane = onehot(iota((16, 128), 1) == 0)
        rim_s[t] = lax.dot_general(first_lane, step, NT, preferred_element_type=f32)[:8]
        for side in range(2):
            for copy in rim_copies(t, side):
                copy.start()

    def rim_copies(t, side):
        peer = rim_peer(side)
        return (
            pltpu.make_async_remote_copy(
                src_ref=rim_s.at[t], dst_ref=got_s.at[side, t],
                send_sem=f_send.at[side, t], recv_sem=f_recv.at[side, t],
                device_id=peer, device_id_type=MESH,
            ),
            pltpu.make_async_remote_copy(
                src_ref=rim_q.at[t], dst_ref=got_q.at[side, t],
                send_sem=q_send.at[side, t], recv_sem=q_recv.at[side, t],
                device_id=peer, device_id_type=MESH,
            ),
        )

    def rim(t, side):
        for copy in rim_copies(t, side):
            copy.wait()
        row = jnp.broadcast_to(got_s[side, t][0:1, :], (128, CELLS)).astype(bf16)
        size = lax.dot_general(eye[...], row, NT, preferred_element_type=f32)
        outside = me_i == (0 if side == 0 else N_IL - 1)
        size = size * jnp.where(outside, 0.0, 1.0)
        base = 0 if side == 0 else 2 * CELLS
        for c in range(w // 128):
            value = got_q[side, t, :, c * 128:(c + 1) * 128].astype(f32)
            ext[base:base + CELLS, t * w + c * 128:t * w + (c + 1) * 128] = value * size

    for t in range(T):
        forward(t)
        if t == 0:
            selector()
        if t > 0:
            stack(t - 1)
    stack(T - 1)
    for t in range(T):
        for side in range(2):
            rim(t, side)


def route(traces, dest, bins, offs):
    n, samples = traces.shape
    w = samples // T
    vmem = pl.BlockSpec(memory_space=pltpu.VMEM)
    dma = pltpu.SemaphoreType.DMA
    return pl.pallas_call(
        route_kernel,
        out_shape=(
            jax.ShapeDtypeStruct((3 * CELLS, samples), f32),
            jax.ShapeDtypeStruct((8, 128), i32),
        ),
        in_specs=[vmem] * 4,
        out_specs=(vmem, vmem),
        scratch_shapes=[
            pltpu.VMEM((8, n), f32),
            pltpu.VMEM((n, n), bf16),
            pltpu.VMEM((N_Z, 128, n), bf16),
            pltpu.VMEM((T, N_Z, POOL, w), bf16),
            pltpu.VMEM((T, N_Z, 128, w), bf16),
            pltpu.VMEM((N_Z, 8, 128), i32),
            pltpu.VMEM((N_Z, 8, 128), i32),
            pltpu.VMEM((16, N_Z * 128), bf16),
            pltpu.VMEM((ROWS, N_Z * 128), bf16),
            pltpu.VMEM((T, N_P, SLOTS, w), bf16),
            pltpu.VMEM((T, N_P, SLOTS, w), bf16),
            pltpu.VMEM((N_P, 8, 128), i32),
            pltpu.VMEM((N_P, 8, 128), i32),
            pltpu.VMEM((8, ROWS), i32),
            pltpu.VMEM((CELLS, ROWS), bf16),
            pltpu.VMEM((CELLS, 128), f32),
            pltpu.VMEM((T, CELLS, w), jnp.int16),
            pltpu.VMEM((T, 8, CELLS), f32),
            pltpu.VMEM((2, T, CELLS, w), jnp.int16),
            pltpu.VMEM((2, T, 8, CELLS), f32),
            dma((T, N_Z)), dma((T, N_Z)), dma((N_Z,)), dma((N_Z,)),
            dma((T, N_P)), dma((T, N_P)), dma((N_P,)), dma((N_P,)),
            dma((2, T)), dma((2, T)), dma((2, T)), dma((2, T)),
        ],
        compiler_params=pltpu.CompilerParams(
            collective_id=0, has_side_effects=True, vmem_limit_bytes=48 * 1024 * 1024
        ),
    )(traces, dest, bins, offs)


def steer(at, dip, samples):
    parts = samples // 128
    lane = iota((8, 128), 1)

    def piece(j, k):
        ref, index = at(j)
        if isinstance(k, int):
            return ref[index + (slice(None), slice(k * 128, (k + 1) * 128))]
        return ref[index + (slice(None), pl.ds(pl.multiple_of(k * 128, 128), 128))]

    def moved(j):
        shift = j * dip
        ahead = jnp.where(shift > 0, 1, 0)
        keep = (lane >= jnp.maximum(shift, 0)) & (lane < 128 + jnp.minimum(shift, 0))
        turn = lax.rem(128 - shift, 128)
        out = []
        for k in range(parts):
            if k == 0:
                other = piece(j, 1) * ahead.astype(f32)
            elif k == parts - 1:
                other = piece(j, k - 1) * (1 - ahead).astype(f32)
            else:
                other = piece(j, k - 1 + 2 * ahead)
            out.append(pltpu.roll(jnp.where(keep, piece(j, k), other), turn, 1))
        return out

    acc = [FILTER_TAPS[4] * piece(0, k) for k in range(parts)]
    for j in (1, 2, 3, 4):
        up, down = moved(j), moved(-j)
        for k in range(parts):
            acc[k] += FILTER_TAPS[4 + j] * (up[k] + down[k])
    return acc


def inline_kernel(dips, ext, out):
    n_il, n_xl, _, samples = out.shape
    base = pl.program_id(0) * n_xl

    def column(x, carry):
        for i in range(n_il):
            acc = steer(lambda j, i=i: (ext, (i + 4 + j, x)), dips[i, base + x], samples)
            for k, part in enumerate(acc):
                out[i, x, :, k * 128:(k + 1) * 128] = part
        return carry

    lax.fori_loop(0, n_xl, column, 0, unroll=2)


def inline_pass(dips, ext):
    n_il, n_xl = dips.shape
    samples = ext.shape[-1]
    step = 4
    return pl.pallas_call(
        inline_kernel,
        grid=(n_xl // step,),
        out_shape=jax.ShapeDtypeStruct((n_il, n_xl, OFFSETS, samples), f32),
        in_specs=[
            pl.BlockSpec(memory_space=pltpu.SMEM),
            pl.BlockSpec((3 * n_il, step, OFFSETS, samples), lambda s: (0, s, 0, 0)),
        ],
        out_specs=pl.BlockSpec((n_il, step, OFFSETS, samples), lambda s: (0, s, 0, 0)),
        compiler_params=pltpu.CompilerParams(vmem_limit_bytes=32 * 1024 * 1024),
    )(dips, ext)


def xline_kernel(dips, left, own, right, out, ext, turned):
    n_xl, samples = own.shape[1], own.shape[3]
    il = pl.program_id(0)
    ext[0:4] = left[0]
    ext[4:4 + n_xl] = own[0]
    ext[4 + n_xl:] = right[0]

    def column(x, carry):
        acc = steer(lambda j: (ext, (x + 4 + j,)), dips[il, x], samples)
        for k, part in enumerate(acc):
            turned[k, pl.ds(x, OFFSETS, stride=n_xl), :] = part
        return carry

    lax.fori_loop(0, n_xl, column, 0, unroll=8)
    for k in range(turned.shape[0]):
        out[:, 0, :, k * 128:(k + 1) * 128] = turned[k].reshape(OFFSETS, n_xl, 128)


def xline_pass(dips, left, own, right):
    n_il, n_xl, _, samples = own.shape
    side = pl.BlockSpec((1, 4, OFFSETS, samples), lambda s: (s, 0, 0, 0))
    return pl.pallas_call(
        xline_kernel,
        grid=(n_il,),
        out_shape=jax.ShapeDtypeStruct((OFFSETS, n_il, n_xl, samples), f32),
        in_specs=[
            pl.BlockSpec(memory_space=pltpu.SMEM),
            side,
            pl.BlockSpec((1, n_xl, OFFSETS, samples), lambda s: (s, 0, 0, 0)),
            side,
        ],
        out_specs=pl.BlockSpec((OFFSETS, 1, n_xl, samples), lambda s: (0, s, 0, 0)),
        scratch_shapes=[
            pltpu.VMEM((n_xl + 8, OFFSETS, samples), f32),
            pltpu.VMEM((samples // 128, OFFSETS * n_xl, 128), f32),
        ],
        compiler_params=pltpu.CompilerParams(vmem_limit_bytes=32 * 1024 * 1024),
    )(dips, left, own, right)


def shifted(cells, axis):
    count = lax.axis_size(axis)
    return (
        lambda tail: lax.ppermute(tail, axis, [(i, i + 1) for i in range(count - 1)]),
        lambda head: lax.ppermute(head, axis, [(i + 1, i) for i in range(count - 1)]),
    )


def padded_2(cells, sides, width):
    for axis, dim in sides:
        count = lax.axis_size(axis)
        ends = count - 1
        head = lax.slice_in_dim(cells, 0, width, axis=dim)
        tail = lax.slice_in_dim(cells, cells.shape[dim] - width, cells.shape[dim], axis=dim)
        cells = jnp.concatenate(
            [
                lax.ppermute(tail, axis, [(i, (i + 1) % count) for i in range(ends)]),
                cells,
                lax.ppermute(head, axis, [((i + 1) % count, i) for i in range(ends)]),
            ],
            axis=dim,
        )
    return cells


def dip_pass(padded, dips, axis, count, samples):
    running = None
    for tap_index in range(9):
        neighbour = lax.slice_in_dim(padded, tap_index, tap_index + count, axis=axis)
        moved = jnp.zeros(neighbour.shape[:-1] + (samples,), jnp.float32)
        for dip_value in range(-dip_limit, dip_limit + 1):
            first_sample = time_pad + (tap_index - 4) * dip_value
            moved = jnp.where(
                (dips == dip_value)[..., None],
                neighbour[..., first_sample : first_sample + samples],
                moved,
            )
        term = FILTER_TAPS[tap_index] * moved
        running = term if running is None else running + term
    return running


def any_load(traces, destination, bin_local, offset_class, dip_inline, dip_xline):
    n_inline = lax.axis_size("inline")
    n_xline = lax.axis_size("xline")
    devices = n_inline * n_xline
    row_count, samples = traces.shape
    capacity = 3 * row_count // devices
    inline_bins, xline_bins = dip_inline.shape
    bin_count = inline_bins * xline_bins
    target = destination[:, 0]
    matches = (target[:, None] == jnp.arange(devices, dtype=jnp.int32)[None, :]).astype(jnp.int32)
    before = jnp.cumsum(matches, axis=0) - matches
    position = jnp.sum(before * matches, axis=1)
    slot_index = target * capacity + position
    labels = offset_class * bin_count + bin_local
    outgoing = jnp.zeros((devices * capacity, samples), jnp.bfloat16).at[slot_index].set(traces)
    outgoing = outgoing.reshape(n_inline, n_xline, capacity, samples)
    out_labels = jnp.full((devices * capacity,), -1, jnp.int32).at[slot_index].set(labels)
    out_labels = out_labels.reshape(n_inline, n_xline, capacity)

    def exchange(value):
        value = lax.all_to_all(value, "inline", split_axis=0, concat_axis=0, tiled=True)
        return lax.all_to_all(value, "xline", split_axis=1, concat_axis=1, tiled=True)

    received = exchange(outgoing).reshape(-1, samples)
    got_labels = exchange(out_labels).reshape(-1)
    cell_total = OFFSETS * bin_count
    selector = jnp.arange(cell_total, dtype=jnp.int32)[:, None] == got_labels[None, :]
    totals = jnp.dot(selector.astype(jnp.bfloat16), received, preferred_element_type=jnp.float32)
    counts = jnp.sum(selector.astype(jnp.int32), axis=1).astype(jnp.float32)
    stacked = (totals / jnp.maximum(counts, 1.0)[:, None]).reshape(
        OFFSETS, inline_bins, xline_bins, samples
    )
    with_rim = padded_2(stacked, (("inline", 1),), 4)
    padded = jnp.pad(with_rim, ((0, 0), (0, 0), (0, 0), (time_pad, time_pad)))
    smoothed = dip_pass(padded, dip_inline, 1, inline_bins, samples)
    with_rim = padded_2(smoothed, (("xline", 2),), 4)
    padded = jnp.pad(with_rim, ((0, 0), (0, 0), (0, 0), (time_pad, time_pad)))
    return dip_pass(padded, dip_xline, 2, xline_bins, samples)


def per_device(traces, destination, bin_local, offset_class, dip_inline, dip_xline):
    n, samples = traces.shape
    n_il, n_xl = dip_inline.shape
    ext, flag = route(
        traces, destination.reshape(1, n), bin_local.reshape(1, n), offset_class.reshape(1, n)
    )
    first = inline_pass(dip_inline, ext.reshape(3 * n_il, n_xl, OFFSETS, samples))
    right, left = shifted(first, "xline")
    from_left = right(first[:, n_xl - 4:])
    from_right = left(first[:, :4])
    return lax.cond(
        flag[0, 0] > 0,
        lambda: any_load(traces, destination, bin_local, offset_class, dip_inline, dip_xline),
        lambda: xline_pass(dip_xline, from_left, first, from_right),
    )


def solution(mesh):
    return jax.shard_map(
        per_device,
        mesh=mesh,
        in_specs=(
            P(("inline", "xline"), None),
            P(("inline", "xline"), None),
            P(("inline", "xline")),
            P(("inline", "xline")),
            P("inline", "xline"),
            P("inline", "xline"),
        ),
        out_specs=P(None, "inline", "xline", None),
        check_vma=False,
    )
```

```python
import jax
import jax.numpy as jnp
from jax import lax
from jax.experimental import pallas as pl
from jax.experimental.pallas import tpu as pltpu
from jax.sharding import PartitionSpec as P

OFFSETS = 8
FILTER_TAPS = (0.05, 0.08, 0.12, 0.15, 0.2, 0.15, 0.12, 0.08, 0.05)
dip_limit = 3
time_pad = 12

MESH = pl.DeviceIdType.MESH
N_Z = 8
N_P = 32
N_XL = 8
N_IL = 32
CAP = 6
POOL = 96
SLOTS = N_Z * CAP
ROWS = N_P * SLOTS
CELLS = 512
BINS = CELLS // OFFSETS
T = 4
NT = (((1,), (1,)), ((), ()))
f32, bf16, i32 = jnp.float32, jnp.bfloat16, jnp.int32


def iota(shape, dim):
    return lax.broadcasted_iota(i32, shape, dim)


def onehot(mask):
    return jnp.where(mask, 1.0, 0.0).astype(bf16)


def steer(at, dip, parts, ks):
    lane = iota((OFFSETS, 128), 1)
    zero = jnp.zeros((OFFSETS, 128), f32)

    def piece(j, k):
        if not 0 <= k < parts:
            return zero
        ref, index = at(j)
        return ref[index + (slice(None), slice(k * 128, (k + 1) * 128))]

    def moved(j):
        shift = j * dip
        after = lane < shift
        before = lane >= 128 + shift
        turn = lax.rem(128 - shift, 128)
        row = [piece(j, k) for k in range(ks[0] - 1, ks[-1] + 2)]
        return [
            pltpu.roll(jnp.where(after, row[i + 2], jnp.where(before, row[i], row[i + 1])), turn, 1)
            for i in range(len(ks))
        ]

    acc = [FILTER_TAPS[4] * piece(0, k) for k in ks]
    for j in (1, 2, 3, 4):
        up, down = moved(j), moved(-j)
        acc = [a + FILTER_TAPS[4 + j] * (u + v) for a, u, v in zip(acc, up, down)]
    return acc


def route_kernel(
    dips, traces, dest, bins, offs, out, flag_out,
    ext, rows, eye, p1, send1, recv1, lab1s, lab1r, l2, p2, send2, recv2, lab2s, lab2r, wide, sel, count,
    rim_q, rim_s, got_q, got_s, edge, got_e,
    s1_send, s1_recv, l1_send, l1_recv, s2_send, s2_recv, l2_send, l2_recv,
    q_send, q_recv, f_send, f_recv, e_send, e_recv,
):
    n, samples = traces.shape
    w = samples // T
    me_i = lax.axis_index("inline")
    me_x = lax.axis_index("xline")
    my_z = lax.rem(me_i, N_Z)
    my_col = me_i // N_Z
    my_p = my_col * N_XL + me_x

    def z_peer(k):
        z = lax.rem(my_z + k, N_Z)
        return z, (my_col * N_Z + z, me_x)

    def p_peer(k):
        p = lax.rem(my_p + k, N_P)
        return p, ((p // N_XL) * N_Z + my_z, lax.rem(p, N_XL))

    def rim_peer(side):
        return (lax.rem(me_i + (1 if side == 0 else N_IL - 1), N_IL), me_x)

    barrier = pltpu.get_barrier_semaphore()
    for side in range(2):
        pl.semaphore_signal(barrier, inc=1, device_id=rim_peer(side), device_id_type=MESH)

    @pl.loop(1, N_Z)
    def _(k):
        pl.semaphore_signal(barrier, inc=1, device_id=z_peer(k)[1], device_id_type=MESH)

    @pl.loop(1, N_P)
    def _(k):
        pl.semaphore_signal(barrier, inc=1, device_id=p_peer(k)[1], device_id_type=MESH)

    d = dest[...]
    eye[...] = onehot(iota((n, n), 0) == iota((n, n), 1))
    wide_d = jnp.broadcast_to(d.astype(f32), (128, n)).astype(bf16)
    dcol = lax.dot_general(eye[...], wide_d, NT, preferred_element_type=f32).astype(i32)
    zcol = (dcol >> 3) & 7
    for t in range(n // 128):
        lanes = slice(t * 128, (t + 1) * 128)
        drow = d[:, lanes]
        earlier = iota((n, 128), 0) < iota((n, 128), 1) + t * 128
        same = (dcol == drow) & earlier
        same_z = (zcol == ((drow >> 3) & 7)) & earlier
        rows[0:1, lanes] = jnp.sum(jnp.where(same, 1.0, 0.0), axis=0, keepdims=True)
        rows[1:2, lanes] = jnp.sum(jnp.where(same_z, 1.0, 0.0), axis=0, keepdims=True)
    position = rows[0:1, :].astype(i32)
    place = rows[1:2, :].astype(i32)
    zrow = (d >> 3) & 7
    plane = (d >> 6) * N_XL + (d & 7)
    over = jnp.max(place, axis=1, keepdims=True) >= POOL
    over = jnp.where(over, 1, 0)
    sub = iota((16, n), 0)
    labels = jnp.where(sub == 0, plane, 0)
    labels = jnp.where(sub == 1, my_z * CAP + position + 1, labels)
    labels = jnp.where(sub == 2, bins[...], labels)
    labels = jnp.where(sub == 3, offs[...], labels)
    labels = labels.astype(f32).astype(bf16)

    @pl.loop(0, N_Z)
    def _(z):
        target = jnp.where(zrow == z, place, -1)
        pick = onehot(iota((128, n), 0) == target)
        p1[z] = pick[:POOL]
        lab = lax.dot_general(labels, pick, NT, preferred_element_type=f32)[:8].astype(i32)
        lab = jnp.where(iota((8, 128), 1) < POOL, lab, 0)
        lab1s[z] = jnp.where(iota((8, 128), 0) == 4, over, lab)

    lab1r[my_z] = lab1s[my_z]

    pl.semaphore_wait(barrier, N_Z - 1 + N_P - 1 + 2)

    def lab1_copy(k):
        z, peer = z_peer(k)
        return pltpu.make_async_remote_copy(
            src_ref=lab1s.at[z], dst_ref=lab1r.at[my_z],
            send_sem=l1_send.at[k], recv_sem=l1_recv.at[k],
            device_id=peer, device_id_type=MESH,
        )

    def row1_copy(t, k):
        z, peer = z_peer(k)
        return pltpu.make_async_remote_copy(
            src_ref=send1.at[t, z], dst_ref=recv1.at[t, my_z],
            send_sem=s1_send.at[t, k], recv_sem=s1_recv.at[t, k],
            device_id=peer, device_id_type=MESH,
        )

    def lab2_copy(k):
        p, peer = p_peer(k)
        return pltpu.make_async_remote_copy(
            src_ref=lab2s.at[p], dst_ref=lab2r.at[my_p],
            send_sem=l2_send.at[k], recv_sem=l2_recv.at[k],
            device_id=peer, device_id_type=MESH,
        )

    def row2_copy(t, k):
        p, peer = p_peer(k)
        return pltpu.make_async_remote_copy(
            src_ref=send2.at[t, p], dst_ref=recv2.at[t, my_p],
            send_sem=s2_send.at[t, k], recv_sem=s2_recv.at[t, k],
            device_id=peer, device_id_type=MESH,
        )

    @pl.loop(1, N_Z)
    def _(k):
        lab1_copy(k).start()

    def send_rows(t):
        picked = jnp.dot(
            p1[...].reshape(N_Z * POOL, n), traces[:, t * w:(t + 1) * w], preferred_element_type=f32
        )
        send1[t] = picked.astype(bf16).reshape(N_Z, POOL, w)

        @pl.loop(1, N_Z)
        def _(k):
            row1_copy(t, k).start()

        recv1[t, my_z] = send1[t, my_z]

    send_rows(0)
    send_rows(1)

    @pl.loop(1, N_Z)
    def _(k):
        lab1_copy(k).wait()

    lab = jnp.concatenate([lab1r[z][:, :POOL] for z in range(N_Z)], axis=1)
    code = lab[1:2, :]
    wide[:, 0:N_Z * POOL] = jnp.where(code > 0, lab[0:1, :] * SLOTS + code - 1, -1) + jnp.zeros_like(lab)
    l2[...] = jnp.concatenate([lab, lab], axis=0).astype(f32).astype(bf16)
    worst = jnp.max(lab[4:5, :], axis=1, keepdims=True)

    @pl.loop(0, N_Z * POOL // 128)
    def _(c):
        lanes = pl.ds(pl.multiple_of(c * 128, 128), 128)
        p2[:, lanes] = onehot(iota((ROWS, 128), 0) == wide[0:1, lanes])

    lab = lax.dot_general(l2[...], p2[...], NT, preferred_element_type=f32).astype(i32)
    cell = jnp.where(lab[1:2, :] > 0, lab[2:3, :] * OFFSETS + lab[3:4, :], -1)
    wide[...] = jnp.where(iota((8, ROWS), 0) == 1, worst, cell)

    @pl.loop(0, N_P // 8)
    def _(g):
        part = wide[:, pl.ds(pl.multiple_of(g * 8 * SLOTS, 128), 8 * SLOTS)]
        for i in range(8):
            lab2s[g * 8 + i, :, 0:SLOTS] = part[:, i * SLOTS:(i + 1) * SLOTS]

    lab2r[my_p] = lab2s[my_p]

    @pl.loop(1, N_P)
    def _(k):
        lab2_copy(k).start()

    def forward(t):
        @pl.loop(1, N_Z)
        def _(k):
            row1_copy(t, k).wait()

        if t + 2 < T:
            send_rows(t + 2)
        arrived = recv1[t].reshape(N_Z * POOL, w)
        half = ROWS // 2
        for g in range(2):
            moved = jnp.dot(p2[g * half:(g + 1) * half, :], arrived, preferred_element_type=f32)
            send2[t, g * (N_P // 2):(g + 1) * (N_P // 2)] = moved.astype(bf16).reshape(N_P // 2, SLOTS, w)

        @pl.loop(1, N_P)
        def _(k):
            row2_copy(t, k).start()

        recv2[t, my_p] = send2[t, my_p]

    def selector():
        @pl.loop(1, N_P)
        def _(k):
            lab2_copy(k).wait()

        @pl.loop(0, N_P // 8)
        def _(g):
            part = jnp.concatenate([lab2r[g * 8 + i][:, 0:SLOTS] for i in range(8)], axis=1)
            wide[:, pl.ds(pl.multiple_of(g * 8 * SLOTS, 128), 8 * SLOTS)] = part

        @pl.loop(0, ROWS // 128)
        def _(c):
            lanes = pl.ds(pl.multiple_of(c * 128, 128), 128)
            sel[:, lanes] = onehot(iota((CELLS, 128), 0) == wide[0:1, lanes])

        traces_per_cell = jnp.dot(sel[...], jnp.ones((ROWS, 128), bf16), preferred_element_type=f32)
        count[...] = jnp.maximum(traces_per_cell, 1.0)
        flag_out[...] = jnp.broadcast_to(jnp.max(wide[1:2, :], axis=1, keepdims=True), (8, 128))

    def stack(t):
        @pl.loop(1, N_P)
        def _(k):
            row2_copy(t, k).wait()

        total = jnp.dot(sel[...], recv2[t].reshape(ROWS, w), preferred_element_type=f32)
        parts = [total[:, c * 128:(c + 1) * 128] / count[...] for c in range(w // 128)]
        top = jnp.abs(parts[0])
        for c, part in enumerate(parts):
            lanes = slice(t * w + c * 128, t * w + (c + 1) * 128)
            ext[BINS:2 * BINS, :, lanes] = part.reshape(BINS, OFFSETS, 128)
            top = jnp.maximum(top, jnp.abs(part))
        step = (jnp.max(top, axis=1, keepdims=True) * (1.01 / 32767.0)).astype(bf16)
        step = jnp.broadcast_to(step, (CELLS, 128))
        size = step.astype(f32)
        fine = jnp.where(size > 0.0, 1.0 / size, 0.0)
        for c, part in enumerate(parts):
            rim_q[t, :, c * 128:(c + 1) * 128] = jnp.round(part * fine).astype(i32).astype(jnp.int16)
        first_lane = onehot(iota((16, 128), 1) == 0)
        rim_s[t] = lax.dot_general(first_lane, step, NT, preferred_element_type=f32)[:8]
        for side in range(2):
            for copy in rim_copies(t, side):
                copy.start()

    def rim_copies(t, side):
        peer = rim_peer(side)
        return (
            pltpu.make_async_remote_copy(
                src_ref=rim_s.at[t], dst_ref=got_s.at[side, t],
                send_sem=f_send.at[side, t], recv_sem=f_recv.at[side, t],
                device_id=peer, device_id_type=MESH,
            ),
            pltpu.make_async_remote_copy(
                src_ref=rim_q.at[t], dst_ref=got_q.at[side, t],
                send_sem=q_send.at[side, t], recv_sem=q_recv.at[side, t],
                device_id=peer, device_id_type=MESH,
            ),
        )

    def rim(t, side):
        for copy in rim_copies(t, side):
            copy.wait()
        row = jnp.broadcast_to(got_s[side, t][0:1, :], (128, CELLS)).astype(bf16)
        size = lax.dot_general(eye[...], row, NT, preferred_element_type=f32)
        outside = me_i == (0 if side == 0 else N_IL - 1)
        size = size * jnp.where(outside, 0.0, 1.0)
        base = 0 if side == 0 else 2 * BINS
        for c in range(w // 128):
            value = got_q[side, t, :, c * 128:(c + 1) * 128].astype(f32)
            lanes = slice(t * w + c * 128, t * w + (c + 1) * 128)
            ext[base:base + BINS, :, lanes] = (value * size).reshape(BINS, OFFSETS, 128)

    n_il, n_xl = dips.shape

    def edge_copy(t, side):
        x = lax.rem(me_x + (1 if side == 0 else N_XL - 1), N_XL)
        return pltpu.make_async_remote_copy(
            src_ref=edge.at[side, t], dst_ref=got_e.at[side, t],
            send_sem=e_send.at[side, t], recv_sem=e_recv.at[side, t],
            device_id=(me_i, x), device_id_type=MESH,
        )

    def inline_pass(t):
        ks = range(t * w // 128, (t + 1) * w // 128)

        def column(x):
            for i in range(n_il):
                acc = steer(lambda j, i=i: (ext, ((i + 4 + j) * n_xl + x,)), dips[i, x], samples // 128, ks)
                for k, part in zip(ks, acc):
                    out[i, x + 4, :, k * 128:(k + 1) * 128] = part

        pl.loop(0, 4)(column)
        pl.loop(n_xl - 4, n_xl)(column)
        lanes = slice(t * w, (t + 1) * w)
        edge[0, t] = out[:, n_xl:n_xl + 4, :, lanes]
        edge[1, t] = out[:, 4:8, :, lanes]
        for side in range(2):
            edge_copy(t, side).start()
        pl.loop(4, n_xl - 4)(column)

    def edges(t):
        lanes = slice(t * w, (t + 1) * w)
        for side in range(2):
            edge_copy(t, side).wait()
            outside = me_x == (0 if side == 0 else N_XL - 1)
            value = got_e[side, t] * jnp.where(outside, 0.0, 1.0)
            if side == 0:
                out[:, 0:4, :, lanes] = value
            else:
                out[:, n_xl + 4:, :, lanes] = value

    def rims(t):
        for side in range(2):
            rim(t, side)

    for t in range(T + 3):
        if t < T:
            forward(t)
        if t == 0:
            selector()
        if 0 <= t - 1 < T:
            stack(t - 1)
        if 0 <= t - 2 < T:
            rims(t - 2)
        if 0 <= t - 3 < T - 1:
            inline_pass(t - 3)
    inline_pass(T - 1)
    for t in range(T):
        edges(t)


def route(dips, traces, dest, bins, offs):
    n, samples = traces.shape
    n_il, n_xl = dips.shape
    w = samples // T
    vmem = pl.BlockSpec(memory_space=pltpu.VMEM)
    dma = pltpu.SemaphoreType.DMA
    return pl.pallas_call(
        route_kernel,
        out_shape=(
            jax.ShapeDtypeStruct((n_il, n_xl + 8, OFFSETS, samples), f32),
            jax.ShapeDtypeStruct((8, 128), i32),
        ),
        in_specs=[pl.BlockSpec(memory_space=pltpu.SMEM)] + [vmem] * 4,
        out_specs=(vmem, vmem),
        scratch_shapes=[
            pltpu.VMEM((3 * BINS, OFFSETS, samples), f32),
            pltpu.VMEM((8, n), f32),
            pltpu.VMEM((n, n), bf16),
            pltpu.VMEM((N_Z, POOL, n), bf16),
            pltpu.VMEM((T, N_Z, POOL, w), bf16),
            pltpu.VMEM((T, N_Z, POOL, w), bf16),
            pltpu.VMEM((N_Z, 8, 128), i32),
            pltpu.VMEM((N_Z, 8, 128), i32),
            pltpu.VMEM((16, N_Z * POOL), bf16),
            pltpu.VMEM((ROWS, N_Z * POOL), bf16),
            pltpu.VMEM((T, N_P, SLOTS, w), bf16),
            pltpu.VMEM((T, N_P, SLOTS, w), bf16),
            pltpu.VMEM((N_P, 8, 128), i32),
            pltpu.VMEM((N_P, 8, 128), i32),
            pltpu.VMEM((8, ROWS), i32),
            pltpu.VMEM((CELLS, ROWS), bf16),
            pltpu.VMEM((CELLS, 128), f32),
            pltpu.VMEM((T, CELLS, w), jnp.int16),
            pltpu.VMEM((T, 8, CELLS), f32),
            pltpu.VMEM((2, T, CELLS, w), jnp.int16),
            pltpu.VMEM((2, T, 8, CELLS), f32),
            pltpu.VMEM((2, T, n_il, 4, OFFSETS, w), f32),
            pltpu.VMEM((2, T, n_il, 4, OFFSETS, w), f32),
            dma((T, N_Z)), dma((T, N_Z)), dma((N_Z,)), dma((N_Z,)),
            dma((T, N_P)), dma((T, N_P)), dma((N_P,)), dma((N_P,)),
            dma((2, T)), dma((2, T)), dma((2, T)), dma((2, T)), dma((2, T)), dma((2, T)),
        ],
        compiler_params=pltpu.CompilerParams(
            collective_id=0, has_side_effects=True, vmem_limit_bytes=48 * 1024 * 1024
        ),
    )(dips, traces, dest, bins, offs)


def xline_kernel(dips, ext, out, turned):
    n_xl, samples = out.shape[2], out.shape[3]
    il = pl.program_id(0)
    ks = range(samples // 128)

    def column(x, carry):
        acc = steer(lambda j: (ext, (0, x + 4 + j)), dips[il, x], len(ks), ks)
        for k, part in zip(ks, acc):
            turned[k, pl.ds(x, OFFSETS, stride=n_xl), :] = part
        return carry

    lax.fori_loop(0, n_xl, column, 0, unroll=8)
    for k in ks:
        out[:, 0, :, k * 128:(k + 1) * 128] = turned[k].reshape(OFFSETS, n_xl, 128)


def xline_pass(dips, ext):
    n_il, n_xl = dips.shape
    samples = ext.shape[-1]
    return pl.pallas_call(
        xline_kernel,
        grid=(n_il,),
        out_shape=jax.ShapeDtypeStruct((OFFSETS, n_il, n_xl, samples), f32),
        in_specs=[
            pl.BlockSpec(memory_space=pltpu.SMEM),
            pl.BlockSpec((1, n_xl + 8, OFFSETS, samples), lambda s: (s, 0, 0, 0)),
        ],
        out_specs=pl.BlockSpec((OFFSETS, 1, n_xl, samples), lambda s: (0, s, 0, 0)),
        scratch_shapes=[pltpu.VMEM((samples // 128, OFFSETS * n_xl, 128), f32)],
        compiler_params=pltpu.CompilerParams(vmem_limit_bytes=60 * 1024 * 1024),
    )(dips, ext)


def padded_2(cells, sides, width):
    for axis, dim in sides:
        count = lax.axis_size(axis)
        ends = count - 1
        head = lax.slice_in_dim(cells, 0, width, axis=dim)
        tail = lax.slice_in_dim(cells, cells.shape[dim] - width, cells.shape[dim], axis=dim)
        cells = jnp.concatenate(
            [
                lax.ppermute(tail, axis, [(i, (i + 1) % count) for i in range(ends)]),
                cells,
                lax.ppermute(head, axis, [((i + 1) % count, i) for i in range(ends)]),
            ],
            axis=dim,
        )
    return cells


def dip_pass(padded, dips, axis, count, samples):
    running = None
    for tap_index in range(9):
        neighbour = lax.slice_in_dim(padded, tap_index, tap_index + count, axis=axis)
        moved = jnp.zeros(neighbour.shape[:-1] + (samples,), jnp.float32)
        for dip_value in range(-dip_limit, dip_limit + 1):
            first_sample = time_pad + (tap_index - 4) * dip_value
            moved = jnp.where(
                (dips == dip_value)[..., None],
                neighbour[..., first_sample : first_sample + samples],
                moved,
            )
        term = FILTER_TAPS[tap_index] * moved
        running = term if running is None else running + term
    return running


def any_load(traces, destination, bin_local, offset_class, dip_inline, dip_xline):
    n_inline = lax.axis_size("inline")
    n_xline = lax.axis_size("xline")
    devices = n_inline * n_xline
    row_count, samples = traces.shape
    capacity = 3 * row_count // devices
    inline_bins, xline_bins = dip_inline.shape
    bin_count = inline_bins * xline_bins
    target = destination[:, 0]
    matches = (target[:, None] == jnp.arange(devices, dtype=jnp.int32)[None, :]).astype(jnp.int32)
    before = jnp.cumsum(matches, axis=0) - matches
    position = jnp.sum(before * matches, axis=1)
    slot_index = target * capacity + position
    labels = offset_class * bin_count + bin_local
    outgoing = jnp.zeros((devices * capacity, samples), jnp.bfloat16).at[slot_index].set(traces)
    outgoing = outgoing.reshape(n_inline, n_xline, capacity, samples)
    out_labels = jnp.full((devices * capacity,), -1, jnp.int32).at[slot_index].set(labels)
    out_labels = out_labels.reshape(n_inline, n_xline, capacity)

    def exchange(value):
        value = lax.all_to_all(value, "inline", split_axis=0, concat_axis=0, tiled=True)
        return lax.all_to_all(value, "xline", split_axis=1, concat_axis=1, tiled=True)

    received = exchange(outgoing).reshape(-1, samples)
    got_labels = exchange(out_labels).reshape(-1)
    cell_total = OFFSETS * bin_count
    selector = jnp.arange(cell_total, dtype=jnp.int32)[:, None] == got_labels[None, :]
    totals = jnp.dot(selector.astype(jnp.bfloat16), received, preferred_element_type=jnp.float32)
    counts = jnp.sum(selector.astype(jnp.int32), axis=1).astype(jnp.float32)
    stacked = (totals / jnp.maximum(counts, 1.0)[:, None]).reshape(
        OFFSETS, inline_bins, xline_bins, samples
    )
    with_rim = padded_2(stacked, (("inline", 1),), 4)
    padded = jnp.pad(with_rim, ((0, 0), (0, 0), (0, 0), (time_pad, time_pad)))
    smoothed = dip_pass(padded, dip_inline, 1, inline_bins, samples)
    with_rim = padded_2(smoothed, (("xline", 2),), 4)
    padded = jnp.pad(with_rim, ((0, 0), (0, 0), (0, 0), (time_pad, time_pad)))
    return dip_pass(padded, dip_xline, 2, xline_bins, samples)


def per_device(traces, destination, bin_local, offset_class, dip_inline, dip_xline):
    n = traces.shape[0]
    first, flag = route(
        dip_inline,
        traces,
        destination.reshape(1, n),
        bin_local.reshape(1, n),
        offset_class.reshape(1, n),
    )
    return lax.cond(
        flag[0, 0] > 0,
        lambda: any_load(traces, destination, bin_local, offset_class, dip_inline, dip_xline),
        lambda: xline_pass(dip_xline, first),
    )


def solution(mesh):
    return jax.shard_map(
        per_device,
        mesh=mesh,
        in_specs=(
            P(("inline", "xline"), None),
            P(("inline", "xline"), None),
            P(("inline", "xline")),
            P(("inline", "xline")),
            P("inline", "xline"),
            P("inline", "xline"),
        ),
        out_specs=P(None, "inline", "xline", None),
        check_vma=False,
    )
```

```python
import jax
import jax.numpy as jnp
from jax import lax
from jax.experimental import pallas as pl
from jax.experimental.pallas import tpu as pltpu
from jax.sharding import PartitionSpec as P

OFFSETS = 8
FILTER_TAPS = (0.05, 0.08, 0.12, 0.15, 0.2, 0.15, 0.12, 0.08, 0.05)
dip_limit = 3
time_pad = 12

MESH = pl.DeviceIdType.MESH
N_Z = 8
N_P = 32
N_XL = 8
N_IL = 32
CAP = 6
POOL = 96
SLOTS = N_Z * CAP
ROWS = N_P * SLOTS
CELLS = 512
BINS = CELLS // OFFSETS
WIDTHS = (128, 256, 256, 256, 128)
STARTS = (0, 128, 384, 640, 896)
T = len(WIDTHS)
W = max(WIDTHS)
UNROLL = 4
NT = (((1,), (1,)), ((), ()))
f32, bf16, i32 = jnp.float32, jnp.bfloat16, jnp.int32


def iota(shape, dim):
    return lax.broadcasted_iota(i32, shape, dim)


def onehot(mask):
    return jnp.where(mask, 1.0, 0.0).astype(bf16)


def steer(at, dip, parts, ks):
    lane = iota((OFFSETS, 128), 1)
    zero = jnp.zeros((OFFSETS, 128), f32)

    def piece(j, k):
        if not 0 <= k < parts:
            return zero
        ref, index = at(j)
        return ref[index + (slice(None), slice(k * 128, (k + 1) * 128))]

    def moved(j):
        shift = j * dip
        after = lane < shift
        before = lane >= 128 + shift
        turn = lax.rem(128 - shift, 128)
        row = [piece(j, k) for k in range(ks[0] - 1, ks[-1] + 2)]
        return [
            pltpu.roll(jnp.where(after, row[i + 2], jnp.where(before, row[i], row[i + 1])), turn, 1)
            for i in range(len(ks))
        ]

    acc = [FILTER_TAPS[4] * piece(0, k) for k in ks]
    for j in (1, 2, 3, 4):
        up, down = moved(j), moved(-j)
        acc = [a + FILTER_TAPS[4 + j] * (u + v) for a, u, v in zip(acc, up, down)]
    return acc


def route_kernel(
    dips, traces_hbm, dest, bins, offs, out_hbm, flag_out,
    traces, out, ext, rows, eye, p1, send1, recv1, lab1s, lab1r, l2, p2, send2, recv2, lab2s, lab2r, wide, sel, share,
    rim_q, rim_s, got_q, got_s, relay, edge, got_e,
    s1_send, s1_recv, l1_send, l1_recv, s2_send, s2_recv, l2_send, l2_recv,
    q_send, q_recv, f_send, f_recv, e_send, e_recv, r_send, r_recv, in_sem, out_sem,
):
    n, samples = traces.shape
    parts = samples // 128

    def span(t):
        return slice(STARTS[t], STARTS[t] + WIDTHS[t])

    def wide_of(t):
        return pl.ds(0, WIDTHS[t])

    me_i = lax.axis_index("inline")
    me_x = lax.axis_index("xline")
    my_z = lax.rem(me_i, N_Z)
    my_col = me_i // N_Z
    my_p = my_col * N_XL + me_x

    def fetch(t):
        return pltpu.make_async_copy(
            traces_hbm.at[:, pl.ds(STARTS[t], WIDTHS[t])], traces.at[:, pl.ds(STARTS[t], WIDTHS[t])], in_sem.at[t]
        )

    def give(t):
        lanes = pl.ds(STARTS[t], WIDTHS[t])
        return pltpu.make_async_copy(out.at[:, :, :, lanes], out_hbm.at[:, :, :, lanes], out_sem.at[t])

    for t in range(T):
        fetch(t).start()

    def z_peer(k):
        z = lax.rem(my_z + k, N_Z)
        return z, (my_col * N_Z + z, me_x)

    def p_peer(k):
        p = lax.rem(my_p + k, N_P)
        return p, ((p // N_XL) * N_Z + my_z, lax.rem(p, N_XL))

    def rim_peer(side):
        return (lax.rem(me_i + (1 if side == 0 else N_IL - 1), N_IL), me_x)

    barrier = pltpu.get_barrier_semaphore()
    for side in range(2):
        pl.semaphore_signal(barrier, inc=1, device_id=rim_peer(side), device_id_type=MESH)

    @pl.loop(1, N_Z)
    def _(k):
        pl.semaphore_signal(barrier, inc=1, device_id=z_peer(k)[1], device_id_type=MESH)

    @pl.loop(1, N_P)
    def _(k):
        pl.semaphore_signal(barrier, inc=1, device_id=p_peer(k)[1], device_id_type=MESH)

    d = dest[...]
    eye[...] = onehot(iota((n, n), 0) == iota((n, n), 1))
    wide_d = jnp.broadcast_to(d.astype(f32), (128, n)).astype(bf16)
    dcol = lax.dot_general(eye[...], wide_d, NT, preferred_element_type=f32).astype(i32)
    zcol = (dcol >> 3) & 7
    for t in range(n // 128):
        lanes = slice(t * 128, (t + 1) * 128)
        drow = d[:, lanes]
        earlier = iota((n, 128), 0) < iota((n, 128), 1) + t * 128
        same = (dcol == drow) & earlier
        same_z = (zcol == ((drow >> 3) & 7)) & earlier
        rows[0:1, lanes] = jnp.sum(jnp.where(same, 1.0, 0.0), axis=0, keepdims=True)
        rows[1:2, lanes] = jnp.sum(jnp.where(same_z, 1.0, 0.0), axis=0, keepdims=True)
    position = rows[0:1, :].astype(i32)
    place = rows[1:2, :].astype(i32)
    zrow = (d >> 3) & 7
    plane = (d >> 6) * N_XL + (d & 7)
    over = jnp.max(place, axis=1, keepdims=True) >= POOL
    over = jnp.where(over, 1, 0)
    sub = iota((16, n), 0)
    labels = jnp.where(sub == 0, plane, 0)
    labels = jnp.where(sub == 1, my_z * CAP + position + 1, labels)
    labels = jnp.where(sub == 2, bins[...], labels)
    labels = jnp.where(sub == 3, offs[...], labels)
    labels = labels.astype(f32).astype(bf16)

    @pl.loop(0, N_Z)
    def _(z):
        target = jnp.where(zrow == z, place, -1)
        pick = onehot(iota((128, n), 0) == target)
        p1[z] = pick[:POOL]
        lab = lax.dot_general(labels, pick, NT, preferred_element_type=f32)[:8].astype(i32)
        lab = jnp.where(iota((8, 128), 1) < POOL, lab, 0)
        lab1s[z] = jnp.where(iota((8, 128), 0) == 4, over, lab)

    lab1r[my_z] = lab1s[my_z]

    pl.semaphore_wait(barrier, N_Z - 1 + N_P - 1 + 2)

    def lab1_copy(k):
        z, peer = z_peer(k)
        return pltpu.make_async_remote_copy(
            src_ref=lab1s.at[z], dst_ref=lab1r.at[my_z],
            send_sem=l1_send.at[k], recv_sem=l1_recv.at[k],
            device_id=peer, device_id_type=MESH,
        )

    def row1_copy(t, k):
        z, peer = z_peer(k)
        return pltpu.make_async_remote_copy(
            src_ref=send1.at[t, z, :, wide_of(t)], dst_ref=recv1.at[t, my_z, :, wide_of(t)],
            send_sem=s1_send.at[t, k], recv_sem=s1_recv.at[t, k],
            device_id=peer, device_id_type=MESH,
        )

    def lab2_copy(k):
        p, peer = p_peer(k)
        return pltpu.make_async_remote_copy(
            src_ref=lab2s.at[p], dst_ref=lab2r.at[my_p],
            send_sem=l2_send.at[k], recv_sem=l2_recv.at[k],
            device_id=peer, device_id_type=MESH,
        )

    def row2_copy(t, k):
        p, peer = p_peer(k)
        return pltpu.make_async_remote_copy(
            src_ref=send2.at[t, p, :, wide_of(t)], dst_ref=recv2.at[t, my_p, :, wide_of(t)],
            send_sem=s2_send.at[t, k], recv_sem=s2_recv.at[t, k],
            device_id=peer, device_id_type=MESH,
        )

    @pl.loop(1, N_Z)
    def _(k):
        lab1_copy(k).start()

    def send_rows(t):
        fetch(t).wait()
        picked = jnp.dot(
            p1[...].reshape(N_Z * POOL, n), traces[:, span(t)], preferred_element_type=f32
        )
        send1[t, :, :, wide_of(t)] = picked.astype(bf16).reshape(N_Z, POOL, WIDTHS[t])

        @pl.loop(1, N_Z)
        def _(k):
            row1_copy(t, k).start()

        recv1[t, my_z, :, wide_of(t)] = send1[t, my_z, :, wide_of(t)]

    send_rows(0)
    send_rows(1)

    @pl.loop(1, N_Z)
    def _(k):
        lab1_copy(k).wait()

    lab = jnp.concatenate([lab1r[z][:, :POOL] for z in range(N_Z)], axis=1)
    code = lab[1:2, :]
    wide[:, 0:N_Z * POOL] = jnp.where(code > 0, lab[0:1, :] * SLOTS + code - 1, -1) + jnp.zeros_like(lab)
    l2[...] = jnp.concatenate([lab, lab], axis=0).astype(f32).astype(bf16)
    worst = jnp.max(lab[4:5, :], axis=1, keepdims=True)

    @pl.loop(0, N_Z * POOL // 128)
    def _(c):
        lanes = pl.ds(pl.multiple_of(c * 128, 128), 128)
        p2[:, lanes] = onehot(iota((ROWS, 128), 0) == wide[0:1, lanes])

    lab = lax.dot_general(l2[...], p2[...], NT, preferred_element_type=f32).astype(i32)
    cell = jnp.where(lab[1:2, :] > 0, lab[2:3, :] * OFFSETS + lab[3:4, :], -1)
    wide[...] = jnp.where(iota((8, ROWS), 0) == 1, worst, cell)

    @pl.loop(0, N_P // 8)
    def _(g):
        part = wide[:, pl.ds(pl.multiple_of(g * 8 * SLOTS, 128), 8 * SLOTS)]
        for i in range(8):
            lab2s[g * 8 + i, :, 0:SLOTS] = part[:, i * SLOTS:(i + 1) * SLOTS]

    lab2r[my_p] = lab2s[my_p]

    @pl.loop(1, N_P)
    def _(k):
        lab2_copy(k).start()

    def forward(t):
        @pl.loop(1, N_Z)
        def _(k):
            row1_copy(t, k).wait()

        if t + 2 < T:
            send_rows(t + 2)
        arrived = recv1[t, :, :, wide_of(t)].reshape(N_Z * POOL, WIDTHS[t])
        half = ROWS // 2
        for g in range(2):
            moved = jnp.dot(p2[g * half:(g + 1) * half, :], arrived, preferred_element_type=f32)
            moved = moved.astype(bf16).reshape(N_P // 2, SLOTS, WIDTHS[t])
            send2[t, g * (N_P // 2):(g + 1) * (N_P // 2), :, wide_of(t)] = moved

        @pl.loop(1, N_P)
        def _(k):
            row2_copy(t, k).start()

        recv2[t, my_p, :, wide_of(t)] = send2[t, my_p, :, wide_of(t)]

    def selector():
        @pl.loop(1, N_P)
        def _(k):
            lab2_copy(k).wait()

        @pl.loop(0, N_P // 8)
        def _(g):
            part = jnp.concatenate([lab2r[g * 8 + i][:, 0:SLOTS] for i in range(8)], axis=1)
            wide[:, pl.ds(pl.multiple_of(g * 8 * SLOTS, 128), 8 * SLOTS)] = part

        @pl.loop(0, ROWS // 128)
        def _(c):
            lanes = pl.ds(pl.multiple_of(c * 128, 128), 128)
            sel[:, lanes] = onehot(iota((CELLS, 128), 0) == wide[0:1, lanes])

        per_cell = jnp.dot(sel[...], jnp.ones((ROWS, 128), bf16), preferred_element_type=f32)
        share[...] = 1.0 / jnp.maximum(per_cell, 1.0)
        flag_out[...] = jnp.broadcast_to(jnp.max(wide[1:2, :], axis=1, keepdims=True), (8, 128))

    def stack(t):
        @pl.loop(1, N_P)
        def _(k):
            row2_copy(t, k).wait()

        total = jnp.dot(sel[...], recv2[t, :, :, wide_of(t)].reshape(ROWS, WIDTHS[t]), preferred_element_type=f32)
        parts = [total[:, c * 128:(c + 1) * 128] * share[...] for c in range(WIDTHS[t] // 128)]
        top = jnp.abs(parts[0])
        for c, part in enumerate(parts):
            lanes = slice(STARTS[t] + c * 128, STARTS[t] + (c + 1) * 128)
            ext[BINS:2 * BINS, :, lanes] = part.reshape(BINS, OFFSETS, 128)
            top = jnp.maximum(top, jnp.abs(part))
        step = (jnp.max(top, axis=1, keepdims=True) * (1.01 / 32767.0)).astype(bf16)
        step = jnp.broadcast_to(step, (CELLS, 128))
        size = step.astype(f32)
        fine = jnp.where(size > 0.0, 1.0 / size, 0.0)
        for c, part in enumerate(parts):
            rim_q[t, :, c * 128:(c + 1) * 128] = jnp.round(part * fine).astype(i32).astype(jnp.int16)
        first_lane = onehot(iota((16, 128), 1) == 0)
        rim_s[t] = lax.dot_general(first_lane, step, NT, preferred_element_type=f32)[:8]
        send_rim(t)

    def size_copy(t, side):
        return pltpu.make_async_remote_copy(
            src_ref=rim_s.at[t], dst_ref=got_s.at[side, t],
            send_sem=f_send.at[side, t], recv_sem=f_recv.at[side, t],
            device_id=rim_peer(side), device_id_type=MESH,
        )

    def rim_copy(t, side, h):
        return pltpu.make_async_remote_copy(
            src_ref=rim_q.at[t, rim_half(h), wide_of(t)], dst_ref=got_q.at[side, t, rim_half(h), wide_of(t)],
            send_sem=q_send.at[side, t, h], recv_sem=q_recv.at[side, t, h],
            device_id=rim_peer(side), device_id_type=MESH,
        )

    def relay_copy(t, side):
        return pltpu.make_async_remote_copy(
            src_ref=rim_q.at[t, rim_half(1), wide_of(t)], dst_ref=relay.at[t, :, wide_of(t)],
            send_sem=q_send.at[side, t, 1], recv_sem=r_recv.at[t],
            device_id=(lax.rem(me_i + (N_Z if side == 0 else N_IL - N_Z), N_IL), me_x), device_id_type=MESH,
        )

    def onward_copy(t, side):
        return pltpu.make_async_remote_copy(
            src_ref=relay.at[t, :, wide_of(t)], dst_ref=got_q.at[side, t, rim_half(1), wide_of(t)],
            send_sem=r_send.at[t], recv_sem=q_recv.at[side, t, 1],
            device_id=(my_col * N_Z + (0 if side == 0 else N_Z - 1), me_x), device_id_type=MESH,
        )

    def rim_half(h):
        return pl.ds(h * CELLS // 2, CELLS // 2)

    def last_plane(side):
        return my_z == (N_Z - 1 if side == 0 else 0)

    def send_rim(t):
        for side in range(2):
            size_copy(t, side).start()
            rim_copy(t, side, 0).start()

            @pl.when(last_plane(side))
            def _():
                relay_copy(t, side).start()

            @pl.when(jnp.logical_not(last_plane(side)))
            def _():
                rim_copy(t, side, 1).start()

    def pass_on(t):
        for side in range(2):
            @pl.when(last_plane(side))
            def _():
                relay_copy(t, side).wait_recv()
                onward_copy(t, side).start()

    def wait_rim(t, side):
        size_copy(t, side).wait()
        rim_copy(t, side, 0).wait()
        rim_copy(t, side, 1).wait()

        @pl.when(last_plane(side))
        def _():
            onward_copy(t, side).wait_send()

    def rim(t, side):
        wait_rim(t, side)
        row = jnp.broadcast_to(got_s[side, t][0:1, :], (128, CELLS)).astype(bf16)
        size = lax.dot_general(eye[...], row, NT, preferred_element_type=f32)
        outside = me_i == (0 if side == 0 else N_IL - 1)
        size = size * jnp.where(outside, 0.0, 1.0)
        base = 0 if side == 0 else 2 * BINS
        for c in range(WIDTHS[t] // 128):
            value = got_q[side, t, :, c * 128:(c + 1) * 128].astype(f32)
            lanes = slice(STARTS[t] + c * 128, STARTS[t] + (c + 1) * 128)
            ext[base:base + BINS, :, lanes] = (value * size).reshape(BINS, OFFSETS, 128)

    n_il, n_xl = dips.shape

    def edge_copy(t, side):
        x = lax.rem(me_x + (1 if side == 0 else N_XL - 1), N_XL)
        return pltpu.make_async_remote_copy(
            src_ref=edge.at[side, t, :, :, :, wide_of(t)], dst_ref=got_e.at[side, t, :, :, :, wide_of(t)],
            send_sem=e_send.at[side, t], recv_sem=e_recv.at[side, t],
            device_id=(me_i, x), device_id_type=MESH,
        )

    def inline_pass(t):
        ks = range(STARTS[t] // 128, (STARTS[t] + WIDTHS[t]) // 128)

        def column(x):
            for i in range(n_il):
                acc = steer(lambda j, i=i: (ext, ((i + 4 + j) * n_xl + x,)), dips[i, x], parts, ks)
                for k, part in zip(ks, acc):
                    out[i, x + 4, :, k * 128:(k + 1) * 128] = part

        pl.loop(0, 4, unroll=UNROLL)(column)
        pl.loop(n_xl - 4, n_xl, unroll=UNROLL)(column)
        edge[0, t, :, :, :, wide_of(t)] = out[:, n_xl:n_xl + 4, :, span(t)]
        edge[1, t, :, :, :, wide_of(t)] = out[:, 4:8, :, span(t)]
        for side in range(2):
            edge_copy(t, side).start()
        pl.loop(4, n_xl - 4, unroll=UNROLL)(column)

    def edges(t):
        lanes = span(t)
        for side in range(2):
            edge_copy(t, side).wait()
            outside = me_x == (0 if side == 0 else N_XL - 1)
            value = got_e[side, t, :, :, :, wide_of(t)] * jnp.where(outside, 0.0, 1.0)
            if side == 0:
                out[:, 0:4, :, lanes] = value
            else:
                out[:, n_xl + 4:, :, lanes] = value
        give(t).start()

    def rims(t):
        for side in range(2):
            rim(t, side)

    for t in range(T + 5):
        if t < T:
            forward(t)
        if t == 0:
            selector()
        if 0 <= t - 2 < T:
            pass_on(t - 2)
        if 0 <= t - 1 < T:
            stack(t - 1)
        if 0 <= t - 3 < T:
            rims(t - 3)
        if 0 <= t - 4 < T:
            inline_pass(t - 4)
        if 0 <= t - 5 < T:
            edges(t - 5)
    for t in range(T):
        give(t).wait()


def route(dips, traces, dest, bins, offs):
    n, samples = traces.shape
    n_il, n_xl = dips.shape
    w = W
    hbm = pl.BlockSpec(memory_space=pltpu.HBM)
    vmem = pl.BlockSpec(memory_space=pltpu.VMEM)
    dma = pltpu.SemaphoreType.DMA
    return pl.pallas_call(
        route_kernel,
        out_shape=(
            jax.ShapeDtypeStruct((n_il, n_xl + 8, OFFSETS, samples), f32),
            jax.ShapeDtypeStruct((8, 128), i32),
        ),
        in_specs=[pl.BlockSpec(memory_space=pltpu.SMEM), hbm] + [vmem] * 3,
        out_specs=(hbm, vmem),
        scratch_shapes=[
            pltpu.VMEM((n, samples), bf16),
            pltpu.VMEM((n_il, n_xl + 8, OFFSETS, samples), f32),
            pltpu.VMEM((3 * BINS, OFFSETS, samples), f32),
            pltpu.VMEM((8, n), f32),
            pltpu.VMEM((n, n), bf16),
            pltpu.VMEM((N_Z, POOL, n), bf16),
            pltpu.VMEM((T, N_Z, POOL, w), bf16),
            pltpu.VMEM((T, N_Z, POOL, w), bf16),
            pltpu.VMEM((N_Z, 8, 128), i32),
            pltpu.VMEM((N_Z, 8, 128), i32),
            pltpu.VMEM((16, N_Z * POOL), bf16),
            pltpu.VMEM((ROWS, N_Z * POOL), bf16),
            pltpu.VMEM((T, N_P, SLOTS, w), bf16),
            pltpu.VMEM((T, N_P, SLOTS, w), bf16),
            pltpu.VMEM((N_P, 8, 128), i32),
            pltpu.VMEM((N_P, 8, 128), i32),
            pltpu.VMEM((8, ROWS), i32),
            pltpu.VMEM((CELLS, ROWS), bf16),
            pltpu.VMEM((CELLS, 128), f32),
            pltpu.VMEM((T, CELLS, w), jnp.int16),
            pltpu.VMEM((T, 8, CELLS), f32),
            pltpu.VMEM((2, T, CELLS, w), jnp.int16),
            pltpu.VMEM((2, T, 8, CELLS), f32),
            pltpu.VMEM((T, CELLS // 2, w), jnp.int16),
            pltpu.VMEM((2, T, n_il, 4, OFFSETS, w), f32),
            pltpu.VMEM((2, T, n_il, 4, OFFSETS, w), f32),
            dma((T, N_Z)), dma((T, N_Z)), dma((N_Z,)), dma((N_Z,)),
            dma((T, N_P)), dma((T, N_P)), dma((N_P,)), dma((N_P,)),
            dma((2, T, 2)), dma((2, T, 2)), dma((2, T)), dma((2, T)), dma((2, T)), dma((2, T)),
            dma((T,)), dma((T,)), dma((T,)), dma((T,)),
        ],
        compiler_params=pltpu.CompilerParams(
            collective_id=0, has_side_effects=True, vmem_limit_bytes=48 * 1024 * 1024
        ),
    )(dips, traces, dest, bins, offs)


def xline_kernel(dips, ext, out, turned):
    n_xl, samples = out.shape[2], out.shape[3]
    il = pl.program_id(0)
    first = pl.program_id(1) * n_xl
    ks = range(samples // 128)

    def column(x, carry):
        acc = steer(lambda j: (ext, (0, first + x + 4 + j)), dips[il, first + x], len(ks), ks)
        for k, part in zip(ks, acc):
            turned[k, pl.ds(x, OFFSETS, stride=n_xl), :] = part
        return carry

    lax.fori_loop(0, n_xl, column, 0, unroll=8)
    for k in ks:
        out[:, 0, :, k * 128:(k + 1) * 128] = turned[k].reshape(OFFSETS, n_xl, 128)


def xline_pass(dips, ext):
    n_il, n_xl = dips.shape
    samples = ext.shape[-1]
    step = n_xl
    return pl.pallas_call(
        xline_kernel,
        grid=(n_il, n_xl // step),
        out_shape=jax.ShapeDtypeStruct((OFFSETS, n_il, n_xl, samples), f32),
        in_specs=[
            pl.BlockSpec(memory_space=pltpu.SMEM),
            pl.BlockSpec((1, n_xl + 8, OFFSETS, samples), lambda s, h: (s, 0, 0, 0)),
        ],
        out_specs=pl.BlockSpec((OFFSETS, 1, step, samples), lambda s, h: (0, s, h, 0)),
        scratch_shapes=[pltpu.VMEM((samples // 128, OFFSETS * step, 128), f32)],
        compiler_params=pltpu.CompilerParams(vmem_limit_bytes=60 * 1024 * 1024),
    )(dips, ext)


def padded_2(cells, sides, width):
    for axis, dim in sides:
        count = lax.axis_size(axis)
        ends = count - 1
        head = lax.slice_in_dim(cells, 0, width, axis=dim)
        tail = lax.slice_in_dim(cells, cells.shape[dim] - width, cells.shape[dim], axis=dim)
        cells = jnp.concatenate(
            [
                lax.ppermute(tail, axis, [(i, (i + 1) % count) for i in range(ends)]),
                cells,
                lax.ppermute(head, axis, [((i + 1) % count, i) for i in range(ends)]),
            ],
            axis=dim,
        )
    return cells


def dip_pass(padded, dips, axis, count, samples):
    running = None
    for tap_index in range(9):
        neighbour = lax.slice_in_dim(padded, tap_index, tap_index + count, axis=axis)
        moved = jnp.zeros(neighbour.shape[:-1] + (samples,), jnp.float32)
        for dip_value in range(-dip_limit, dip_limit + 1):
            first_sample = time_pad + (tap_index - 4) * dip_value
            moved = jnp.where(
                (dips == dip_value)[..., None],
                neighbour[..., first_sample : first_sample + samples],
                moved,
            )
        term = FILTER_TAPS[tap_index] * moved
        running = term if running is None else running + term
    return running


def any_load(traces, destination, bin_local, offset_class, dip_inline, dip_xline):
    n_inline = lax.axis_size("inline")
    n_xline = lax.axis_size("xline")
    devices = n_inline * n_xline
    row_count, samples = traces.shape
    capacity = 3 * row_count // devices
    inline_bins, xline_bins = dip_inline.shape
    bin_count = inline_bins * xline_bins
    target = destination[:, 0]
    matches = (target[:, None] == jnp.arange(devices, dtype=jnp.int32)[None, :]).astype(jnp.int32)
    before = jnp.cumsum(matches, axis=0) - matches
    position = jnp.sum(before * matches, axis=1)
    slot_index = target * capacity + position
    labels = offset_class * bin_count + bin_local
    outgoing = jnp.zeros((devices * capacity, samples), jnp.bfloat16).at[slot_index].set(traces)
    outgoing = outgoing.reshape(n_inline, n_xline, capacity, samples)
    out_labels = jnp.full((devices * capacity,), -1, jnp.int32).at[slot_index].set(labels)
    out_labels = out_labels.reshape(n_inline, n_xline, capacity)

    def exchange(value):
        value = lax.all_to_all(value, "inline", split_axis=0, concat_axis=0, tiled=True)
        return lax.all_to_all(value, "xline", split_axis=1, concat_axis=1, tiled=True)

    received = exchange(outgoing).reshape(-1, samples)
    got_labels = exchange(out_labels).reshape(-1)
    cell_total = OFFSETS * bin_count
    selector = jnp.arange(cell_total, dtype=jnp.int32)[:, None] == got_labels[None, :]
    totals = jnp.dot(selector.astype(jnp.bfloat16), received, preferred_element_type=jnp.float32)
    counts = jnp.sum(selector.astype(jnp.int32), axis=1).astype(jnp.float32)
    stacked = (totals / jnp.maximum(counts, 1.0)[:, None]).reshape(
        OFFSETS, inline_bins, xline_bins, samples
    )
    with_rim = padded_2(stacked, (("inline", 1),), 4)
    padded = jnp.pad(with_rim, ((0, 0), (0, 0), (0, 0), (time_pad, time_pad)))
    smoothed = dip_pass(padded, dip_inline, 1, inline_bins, samples)
    with_rim = padded_2(smoothed, (("xline", 2),), 4)
    padded = jnp.pad(with_rim, ((0, 0), (0, 0), (0, 0), (time_pad, time_pad)))
    return dip_pass(padded, dip_xline, 2, xline_bins, samples)


def per_device(traces, destination, bin_local, offset_class, dip_inline, dip_xline):
    n = traces.shape[0]
    first, flag = route(
        dip_inline,
        traces,
        destination.reshape(1, n),
        bin_local.reshape(1, n),
        offset_class.reshape(1, n),
    )
    return lax.cond(
        flag[0, 0] > 0,
        lambda: any_load(traces, destination, bin_local, offset_class, dip_inline, dip_xline),
        lambda: xline_pass(dip_xline, first),
    )


def solution(mesh):
    return jax.shard_map(
        per_device,
        mesh=mesh,
        in_specs=(
            P(("inline", "xline"), None),
            P(("inline", "xline"), None),
            P(("inline", "xline")),
            P(("inline", "xline")),
            P("inline", "xline"),
            P("inline", "xline"),
        ),
        out_specs=P(None, "inline", "xline", None),
        check_vma=False,
    )
```

```python
import jax
import jax.numpy as jnp
from jax import lax
from jax.experimental import pallas as pl
from jax.experimental.pallas import tpu as pltpu
from jax.sharding import PartitionSpec as P

OFFSETS = 8
FILTER_TAPS = (0.05, 0.08, 0.12, 0.15, 0.2, 0.15, 0.12, 0.08, 0.05)
dip_limit = 3
time_pad = 12

MESH = pl.DeviceIdType.MESH
N_Z = 8
N_P = 32
N_XL = 8
N_IL = 32
CAP = 6
POOL = 96
SLOTS = N_Z * CAP
ROWS = N_P * SLOTS
CELLS = 512
BINS = CELLS // OFFSETS
WIDTHS = (128, 256, 256, 256, 128)
STARTS = (0, 128, 384, 640, 896)
T = len(WIDTHS)
W = max(WIDTHS)
UNROLL = 4
NT = (((1,), (1,)), ((), ()))
f32, bf16, i32 = jnp.float32, jnp.bfloat16, jnp.int32


def iota(shape, dim):
    return lax.broadcasted_iota(i32, shape, dim)


def onehot(mask):
    return jnp.where(mask, 1.0, 0.0).astype(bf16)


def steer(at, dip, parts, ks):
    lane = iota((OFFSETS, 128), 1)
    zero = jnp.zeros((OFFSETS, 128), f32)

    def piece(j, k):
        if not 0 <= k < parts:
            return zero
        ref, index = at(j)
        return ref[index + (slice(None), slice(k * 128, (k + 1) * 128))]

    def moved(j):
        shift = j * dip
        after = lane < shift
        before = lane >= 128 + shift
        turn = lax.rem(128 - shift, 128)
        row = [piece(j, k) for k in range(ks[0] - 1, ks[-1] + 2)]
        return [
            pltpu.roll(jnp.where(after, row[i + 2], jnp.where(before, row[i], row[i + 1])), turn, 1)
            for i in range(len(ks))
        ]

    acc = [FILTER_TAPS[4] * piece(0, k) for k in ks]
    for j in (1, 2, 3, 4):
        up, down = moved(j), moved(-j)
        acc = [a + FILTER_TAPS[4 + j] * (u + v) for a, u, v in zip(acc, up, down)]
    return acc


def route_kernel(
    dips, traces_hbm, dest, bins, offs, out_hbm, flag_out,
    traces, out, ext, rows, eye, p1, send1, recv1, lab1s, lab1r, l2, p2, send2, recv2, lab2s, lab2r, wide, sel, share,
    rim_q, rim_s, got_q, got_s, relay, edge, got_e,
    s1_send, s1_recv, l1_send, l1_recv, s2_send, s2_recv, l2_send, l2_recv,
    q_send, q_recv, f_send, f_recv, e_send, e_recv, r_send, r_recv, in_sem, out_sem,
):
    n, samples = traces.shape
    parts = samples // 128

    def span(t):
        return slice(STARTS[t], STARTS[t] + WIDTHS[t])

    def wide_of(t):
        return pl.ds(0, WIDTHS[t])

    me_i = lax.axis_index("inline")
    me_x = lax.axis_index("xline")
    my_z = lax.rem(me_i, N_Z)
    my_col = me_i // N_Z
    my_p = my_col * N_XL + me_x

    def fetch(t):
        return pltpu.make_async_copy(
            traces_hbm.at[:, pl.ds(STARTS[t], WIDTHS[t])], traces.at[:, pl.ds(STARTS[t], WIDTHS[t])], in_sem.at[t]
        )

    def give(t):
        lanes = pl.ds(STARTS[t], WIDTHS[t])
        return pltpu.make_async_copy(out.at[:, :, :, lanes], out_hbm.at[:, :, :, lanes], out_sem.at[t])

    for t in range(T):
        fetch(t).start()

    def z_peer(k):
        z = lax.rem(my_z + k, N_Z)
        return z, (my_col * N_Z + z, me_x)

    def p_peer(k):
        p = lax.rem(my_p + k, N_P)
        return p, ((p // N_XL) * N_Z + my_z, lax.rem(p, N_XL))

    def rim_peer(side):
        return (lax.rem(me_i + (1 if side == 0 else N_IL - 1), N_IL), me_x)

    barrier = pltpu.get_barrier_semaphore()
    for side in range(2):
        pl.semaphore_signal(barrier, inc=1, device_id=rim_peer(side), device_id_type=MESH)

    @pl.loop(1, N_Z)
    def _(k):
        pl.semaphore_signal(barrier, inc=1, device_id=z_peer(k)[1], device_id_type=MESH)

    @pl.loop(1, N_P)
    def _(k):
        pl.semaphore_signal(barrier, inc=1, device_id=p_peer(k)[1], device_id_type=MESH)

    d = dest[...]
    eye[...] = onehot(iota((n, n), 0) == iota((n, n), 1))
    wide_d = jnp.broadcast_to(d.astype(f32), (128, n)).astype(bf16)
    dcol = lax.dot_general(eye[...], wide_d, NT, preferred_element_type=f32).astype(i32)
    zcol = (dcol >> 3) & 7
    for t in range(n // 128):
        lanes = slice(t * 128, (t + 1) * 128)
        drow = d[:, lanes]
        earlier = iota((n, 128), 0) < iota((n, 128), 1) + t * 128
        same = (dcol == drow) & earlier
        same_z = (zcol == ((drow >> 3) & 7)) & earlier
        rows[0:1, lanes] = jnp.sum(jnp.where(same, 1.0, 0.0), axis=0, keepdims=True)
        rows[1:2, lanes] = jnp.sum(jnp.where(same_z, 1.0, 0.0), axis=0, keepdims=True)
    position = rows[0:1, :].astype(i32)
    place = rows[1:2, :].astype(i32)
    zrow = (d >> 3) & 7
    plane = (d >> 6) * N_XL + (d & 7)
    over = jnp.max(place, axis=1, keepdims=True) >= POOL
    over = jnp.where(over, 1, 0)
    sub = iota((16, n), 0)
    labels = jnp.where(sub == 0, plane, 0)
    labels = jnp.where(sub == 1, my_z * CAP + position + 1, labels)
    labels = jnp.where(sub == 2, bins[...], labels)
    labels = jnp.where(sub == 3, offs[...], labels)
    labels = labels.astype(f32).astype(bf16)

    @pl.loop(0, N_Z)
    def _(z):
        target = jnp.where(zrow == z, place, -1)
        pick = onehot(iota((128, n), 0) == target)
        p1[z] = pick[:POOL]
        lab = lax.dot_general(labels, pick, NT, preferred_element_type=f32)[:8].astype(i32)
        lab = jnp.where(iota((8, 128), 1) < POOL, lab, 0)
        lab1s[z] = jnp.where(iota((8, 128), 0) == 4, over, lab)

    lab1r[my_z] = lab1s[my_z]

    pl.semaphore_wait(barrier, N_Z - 1 + N_P - 1 + 2)

    def lab1_copy(k):
        z, peer = z_peer(k)
        return pltpu.make_async_remote_copy(
            src_ref=lab1s.at[z], dst_ref=lab1r.at[my_z],
            send_sem=l1_send.at[0], recv_sem=l1_recv.at[0],
            device_id=peer, device_id_type=MESH,
        )

    def row1_copy(t, k):
        z, peer = z_peer(k)
        return pltpu.make_async_remote_copy(
            src_ref=send1.at[t, z, :, wide_of(t)], dst_ref=recv1.at[t, my_z, :, wide_of(t)],
            send_sem=s1_send.at[t], recv_sem=s1_recv.at[t],
            device_id=peer, device_id_type=MESH,
        )

    def lab2_copy(k):
        p, peer = p_peer(k)
        return pltpu.make_async_remote_copy(
            src_ref=lab2s.at[p], dst_ref=lab2r.at[my_p],
            send_sem=l2_send.at[0], recv_sem=l2_recv.at[0],
            device_id=peer, device_id_type=MESH,
        )

    def row2_copy(t, k):
        p, peer = p_peer(k)
        return pltpu.make_async_remote_copy(
            src_ref=send2.at[t, p, :, wide_of(t)], dst_ref=recv2.at[t, my_p, :, wide_of(t)],
            send_sem=s2_send.at[t], recv_sem=s2_recv.at[t],
            device_id=peer, device_id_type=MESH,
        )

    def all_of(src, dst, send, recv, peer):
        return pltpu.make_async_remote_copy(
            src_ref=src, dst_ref=dst, send_sem=send, recv_sem=recv, device_id=peer, device_id_type=MESH
        )

    z_others, p_others = pl.ds(0, N_Z - 1), pl.ds(0, N_P - 1)
    lab1_all = all_of(lab1s.at[z_others], lab1r.at[z_others], l1_send.at[0], l1_recv.at[0], z_peer(1)[1])
    lab2_all = all_of(lab2s.at[p_others], lab2r.at[p_others], l2_send.at[0], l2_recv.at[0], p_peer(1)[1])

    def row1_all(t):
        return all_of(
            send1.at[t, z_others, :, wide_of(t)], recv1.at[t, z_others, :, wide_of(t)],
            s1_send.at[t], s1_recv.at[t], z_peer(1)[1],
        )

    def row2_all(t):
        return all_of(
            send2.at[t, p_others, :, wide_of(t)], recv2.at[t, p_others, :, wide_of(t)],
            s2_send.at[t], s2_recv.at[t], p_peer(1)[1],
        )

    @pl.loop(1, N_Z)
    def _(k):
        lab1_copy(k).start()

    def send_rows(t):
        fetch(t).wait()
        picked = jnp.dot(
            p1[...].reshape(N_Z * POOL, n), traces[:, span(t)], preferred_element_type=f32
        )
        send1[t, :, :, wide_of(t)] = picked.astype(bf16).reshape(N_Z, POOL, WIDTHS[t])

        @pl.loop(1, N_Z)
        def _(k):
            row1_copy(t, k).start()

        recv1[t, my_z, :, wide_of(t)] = send1[t, my_z, :, wide_of(t)]

    send_rows(0)
    send_rows(1)

    lab1_all.wait_recv()

    lab = jnp.concatenate([lab1r[z][:, :POOL] for z in range(N_Z)], axis=1)
    code = lab[1:2, :]
    wide[:, 0:N_Z * POOL] = jnp.where(code > 0, lab[0:1, :] * SLOTS + code - 1, -1) + jnp.zeros_like(lab)
    l2[...] = jnp.concatenate([lab, lab], axis=0).astype(f32).astype(bf16)
    worst = jnp.max(lab[4:5, :], axis=1, keepdims=True)

    @pl.loop(0, N_Z * POOL // 128)
    def _(c):
        lanes = pl.ds(pl.multiple_of(c * 128, 128), 128)
        p2[:, lanes] = onehot(iota((ROWS, 128), 0) == wide[0:1, lanes])

    lab = lax.dot_general(l2[...], p2[...], NT, preferred_element_type=f32).astype(i32)
    cell = jnp.where(lab[1:2, :] > 0, lab[2:3, :] * OFFSETS + lab[3:4, :], -1)
    wide[...] = jnp.where(iota((8, ROWS), 0) == 1, worst, cell)

    @pl.loop(0, N_P // 8)
    def _(g):
        part = wide[:, pl.ds(pl.multiple_of(g * 8 * SLOTS, 128), 8 * SLOTS)]
        for i in range(8):
            lab2s[g * 8 + i, :, 0:SLOTS] = part[:, i * SLOTS:(i + 1) * SLOTS]

    lab2r[my_p] = lab2s[my_p]

    @pl.loop(1, N_P)
    def _(k):
        lab2_copy(k).start()

    def forward(t):
        row1_all(t).wait_recv()

        if t + 2 < T:
            send_rows(t + 2)
        arrived = recv1[t, :, :, wide_of(t)].reshape(N_Z * POOL, WIDTHS[t])
        half = ROWS // 2
        for g in range(2):
            moved = jnp.dot(p2[g * half:(g + 1) * half, :], arrived, preferred_element_type=f32)
            moved = moved.astype(bf16).reshape(N_P // 2, SLOTS, WIDTHS[t])
            send2[t, g * (N_P // 2):(g + 1) * (N_P // 2), :, wide_of(t)] = moved

        @pl.loop(1, N_P)
        def _(k):
            row2_copy(t, k).start()

        recv2[t, my_p, :, wide_of(t)] = send2[t, my_p, :, wide_of(t)]

    def selector():
        lab2_all.wait_recv()
        lab1_all.wait_send()

        @pl.loop(0, N_P // 8)
        def _(g):
            part = jnp.concatenate([lab2r[g * 8 + i][:, 0:SLOTS] for i in range(8)], axis=1)
            wide[:, pl.ds(pl.multiple_of(g * 8 * SLOTS, 128), 8 * SLOTS)] = part

        @pl.loop(0, ROWS // 128)
        def _(c):
            lanes = pl.ds(pl.multiple_of(c * 128, 128), 128)
            sel[:, lanes] = onehot(iota((CELLS, 128), 0) == wide[0:1, lanes])

        per_cell = jnp.dot(sel[...], jnp.ones((ROWS, 128), bf16), preferred_element_type=f32)
        share[...] = 1.0 / jnp.maximum(per_cell, 1.0)
        flag_out[...] = jnp.broadcast_to(jnp.max(wide[1:2, :], axis=1, keepdims=True), (8, 128))

    def stack(t):
        row2_all(t).wait_recv()

        total = jnp.dot(sel[...], recv2[t, :, :, wide_of(t)].reshape(ROWS, WIDTHS[t]), preferred_element_type=f32)
        parts = [total[:, c * 128:(c + 1) * 128] * share[...] for c in range(WIDTHS[t] // 128)]
        top = jnp.abs(parts[0])
        for c, part in enumerate(parts):
            lanes = slice(STARTS[t] + c * 128, STARTS[t] + (c + 1) * 128)
            ext[BINS:2 * BINS, :, lanes] = part.reshape(BINS, OFFSETS, 128)
            top = jnp.maximum(top, jnp.abs(part))
        step = (jnp.max(top, axis=1, keepdims=True) * (1.01 / 32767.0)).astype(bf16)
        step = jnp.broadcast_to(step, (CELLS, 128))
        size = step.astype(f32)
        fine = jnp.where(size > 0.0, 1.0 / size, 0.0)
        for c, part in enumerate(parts):
            rim_q[t, :, c * 128:(c + 1) * 128] = jnp.round(part * fine).astype(i32).astype(jnp.int16)
        first_lane = onehot(iota((16, 128), 1) == 0)
        rim_s[t] = lax.dot_general(first_lane, step, NT, preferred_element_type=f32)[:8]
        send_rim(t)

    def size_copy(t, side):
        return pltpu.make_async_remote_copy(
            src_ref=rim_s.at[t], dst_ref=got_s.at[side, t],
            send_sem=f_send.at[side, t], recv_sem=f_recv.at[side, t],
            device_id=rim_peer(side), device_id_type=MESH,
        )

    def rim_copy(t, side, h):
        return pltpu.make_async_remote_copy(
            src_ref=rim_q.at[t, rim_half(h), wide_of(t)], dst_ref=got_q.at[side, t, rim_half(h), wide_of(t)],
            send_sem=q_send.at[side, t, h], recv_sem=q_recv.at[side, t, h],
            device_id=rim_peer(side), device_id_type=MESH,
        )

    def relay_copy(t, side):
        return pltpu.make_async_remote_copy(
            src_ref=rim_q.at[t, rim_half(1), wide_of(t)], dst_ref=relay.at[t, :, wide_of(t)],
            send_sem=q_send.at[side, t, 1], recv_sem=r_recv.at[t],
            device_id=(lax.rem(me_i + (N_Z if side == 0 else N_IL - N_Z), N_IL), me_x), device_id_type=MESH,
        )

    def onward_copy(t, side):
        return pltpu.make_async_remote_copy(
            src_ref=relay.at[t, :, wide_of(t)], dst_ref=got_q.at[side, t, rim_half(1), wide_of(t)],
            send_sem=r_send.at[t], recv_sem=q_recv.at[side, t, 1],
            device_id=(my_col * N_Z + (0 if side == 0 else N_Z - 1), me_x), device_id_type=MESH,
        )

    def rim_half(h):
        return pl.ds(h * CELLS // 2, CELLS // 2)

    def last_plane(side):
        return my_z == (N_Z - 1 if side == 0 else 0)

    def send_rim(t):
        for side in range(2):
            size_copy(t, side).start()
            rim_copy(t, side, 0).start()

            @pl.when(last_plane(side))
            def _():
                relay_copy(t, side).start()

            @pl.when(jnp.logical_not(last_plane(side)))
            def _():
                rim_copy(t, side, 1).start()

    def pass_on(t):
        for side in range(2):
            @pl.when(last_plane(side))
            def _():
                relay_copy(t, side).wait_recv()
                onward_copy(t, side).start()

    def wait_rim(t, side):
        size_copy(t, side).wait_recv()
        rim_copy(t, side, 0).wait_recv()
        rim_copy(t, side, 1).wait_recv()

    def sent(t):
        row1_all(t).wait_send()
        row2_all(t).wait_send()
        for side in range(2):
            size_copy(t, side).wait_send()
            rim_copy(t, side, 0).wait_send()
            rim_copy(t, side, 1).wait_send()

            @pl.when(last_plane(side))
            def _():
                onward_copy(t, side).wait_send()

    def rim(t, side):
        wait_rim(t, side)
        row = jnp.broadcast_to(got_s[side, t][0:1, :], (128, CELLS)).astype(bf16)
        size = lax.dot_general(eye[...], row, NT, preferred_element_type=f32)
        outside = me_i == (0 if side == 0 else N_IL - 1)
        size = size * jnp.where(outside, 0.0, 1.0)
        base = 0 if side == 0 else 2 * BINS
        for c in range(WIDTHS[t] // 128):
            value = got_q[side, t, :, c * 128:(c + 1) * 128].astype(f32)
            lanes = slice(STARTS[t] + c * 128, STARTS[t] + (c + 1) * 128)
            ext[base:base + BINS, :, lanes] = (value * size).reshape(BINS, OFFSETS, 128)

    n_il, n_xl = dips.shape

    def edge_copy(t, side):
        x = lax.rem(me_x + (1 if side == 0 else N_XL - 1), N_XL)
        return pltpu.make_async_remote_copy(
            src_ref=edge.at[side, t, :, :, :, wide_of(t)], dst_ref=got_e.at[side, t, :, :, :, wide_of(t)],
            send_sem=e_send.at[side, t], recv_sem=e_recv.at[side, t],
            device_id=(me_i, x), device_id_type=MESH,
        )

    def inline_pass(t):
        ks = range(STARTS[t] // 128, (STARTS[t] + WIDTHS[t]) // 128)

        def column(x):
            for i in range(n_il):
                acc = steer(lambda j, i=i: (ext, ((i + 4 + j) * n_xl + x,)), dips[i, x], parts, ks)
                for k, part in zip(ks, acc):
                    out[i, x + 4, :, k * 128:(k + 1) * 128] = part

        pl.loop(0, 4, unroll=UNROLL)(column)
        pl.loop(n_xl - 4, n_xl, unroll=UNROLL)(column)
        edge[0, t, :, :, :, wide_of(t)] = out[:, n_xl:n_xl + 4, :, span(t)]
        edge[1, t, :, :, :, wide_of(t)] = out[:, 4:8, :, span(t)]
        for side in range(2):
            edge_copy(t, side).start()
        pl.loop(4, n_xl - 4, unroll=UNROLL)(column)

    def edges(t):
        lanes = span(t)
        for side in range(2):
            edge_copy(t, side).wait()
            outside = me_x == (0 if side == 0 else N_XL - 1)
            value = got_e[side, t, :, :, :, wide_of(t)] * jnp.where(outside, 0.0, 1.0)
            if side == 0:
                out[:, 0:4, :, lanes] = value
            else:
                out[:, n_xl + 4:, :, lanes] = value
        give(t).start()
        sent(t)

    def rims(t):
        for side in range(2):
            rim(t, side)

    for t in range(T + 5):
        if t < T:
            forward(t)
        if t == 0:
            selector()
        if 0 <= t - 2 < T:
            pass_on(t - 2)
        if 0 <= t - 1 < T:
            stack(t - 1)
        if 0 <= t - 3 < T:
            rims(t - 3)
        if 0 <= t - 4 < T:
            inline_pass(t - 4)
        if 0 <= t - 5 < T:
            edges(t - 5)
    lab2_all.wait_send()
    for t in range(T):
        give(t).wait()


def route(dips, traces, dest, bins, offs):
    n, samples = traces.shape
    n_il, n_xl = dips.shape
    w = W
    hbm = pl.BlockSpec(memory_space=pltpu.HBM)
    vmem = pl.BlockSpec(memory_space=pltpu.VMEM)
    dma = pltpu.SemaphoreType.DMA
    return pl.pallas_call(
        route_kernel,
        out_shape=(
            jax.ShapeDtypeStruct((n_il, n_xl + 8, OFFSETS, samples), f32),
            jax.ShapeDtypeStruct((8, 128), i32),
        ),
        in_specs=[pl.BlockSpec(memory_space=pltpu.SMEM), hbm] + [vmem] * 3,
        out_specs=(hbm, vmem),
        scratch_shapes=[
            pltpu.VMEM((n, samples), bf16),
            pltpu.VMEM((n_il, n_xl + 8, OFFSETS, samples), f32),
            pltpu.VMEM((3 * BINS, OFFSETS, samples), f32),
            pltpu.VMEM((8, n), f32),
            pltpu.VMEM((n, n), bf16),
            pltpu.VMEM((N_Z, POOL, n), bf16),
            pltpu.VMEM((T, N_Z, POOL, w), bf16),
            pltpu.VMEM((T, N_Z, POOL, w), bf16),
            pltpu.VMEM((N_Z, 8, 128), i32),
            pltpu.VMEM((N_Z, 8, 128), i32),
            pltpu.VMEM((16, N_Z * POOL), bf16),
            pltpu.VMEM((ROWS, N_Z * POOL), bf16),
            pltpu.VMEM((T, N_P, SLOTS, w), bf16),
            pltpu.VMEM((T, N_P, SLOTS, w), bf16),
            pltpu.VMEM((N_P, 8, 128), i32),
            pltpu.VMEM((N_P, 8, 128), i32),
            pltpu.VMEM((8, ROWS), i32),
            pltpu.VMEM((CELLS, ROWS), bf16),
            pltpu.VMEM((CELLS, 128), f32),
            pltpu.VMEM((T, CELLS, w), jnp.int16),
            pltpu.VMEM((T, 8, CELLS), f32),
            pltpu.VMEM((2, T, CELLS, w), jnp.int16),
            pltpu.VMEM((2, T, 8, CELLS), f32),
            pltpu.VMEM((T, CELLS // 2, w), jnp.int16),
            pltpu.VMEM((2, T, n_il, 4, OFFSETS, w), f32),
            pltpu.VMEM((2, T, n_il, 4, OFFSETS, w), f32),
            dma((T,)), dma((T,)), dma((1,)), dma((1,)),
            dma((T,)), dma((T,)), dma((1,)), dma((1,)),
            dma((2, T, 2)), dma((2, T, 2)), dma((2, T)), dma((2, T)), dma((2, T)), dma((2, T)),
            dma((T,)), dma((T,)), dma((T,)), dma((T,)),
        ],
        compiler_params=pltpu.CompilerParams(
            collective_id=0, has_side_effects=True, vmem_limit_bytes=48 * 1024 * 1024
        ),
    )(dips, traces, dest, bins, offs)


def xline_kernel(dips, ext, out, turned):
    n_xl, samples = out.shape[2], out.shape[3]
    il = pl.program_id(0)
    first = pl.program_id(1) * n_xl
    ks = range(samples // 128)

    def column(x, carry):
        acc = steer(lambda j: (ext, (0, first + x + 4 + j)), dips[il, first + x], len(ks), ks)
        for k, part in zip(ks, acc):
            turned[k, pl.ds(x, OFFSETS, stride=n_xl), :] = part
        return carry

    lax.fori_loop(0, n_xl, column, 0, unroll=8)
    for k in ks:
        out[:, 0, :, k * 128:(k + 1) * 128] = turned[k].reshape(OFFSETS, n_xl, 128)


def xline_pass(dips, ext):
    n_il, n_xl = dips.shape
    samples = ext.shape[-1]
    step = n_xl
    return pl.pallas_call(
        xline_kernel,
        grid=(n_il, n_xl // step),
        out_shape=jax.ShapeDtypeStruct((OFFSETS, n_il, n_xl, samples), f32),
        in_specs=[
            pl.BlockSpec(memory_space=pltpu.SMEM),
            pl.BlockSpec((1, n_xl + 8, OFFSETS, samples), lambda s, h: (s, 0, 0, 0)),
        ],
        out_specs=pl.BlockSpec((OFFSETS, 1, step, samples), lambda s, h: (0, s, h, 0)),
        scratch_shapes=[pltpu.VMEM((samples // 128, OFFSETS * step, 128), f32)],
        compiler_params=pltpu.CompilerParams(vmem_limit_bytes=60 * 1024 * 1024),
    )(dips, ext)


def padded_2(cells, sides, width):
    for axis, dim in sides:
        count = lax.axis_size(axis)
        ends = count - 1
        head = lax.slice_in_dim(cells, 0, width, axis=dim)
        tail = lax.slice_in_dim(cells, cells.shape[dim] - width, cells.shape[dim], axis=dim)
        cells = jnp.concatenate(
            [
                lax.ppermute(tail, axis, [(i, (i + 1) % count) for i in range(ends)]),
                cells,
                lax.ppermute(head, axis, [((i + 1) % count, i) for i in range(ends)]),
            ],
            axis=dim,
        )
    return cells


def dip_pass(padded, dips, axis, count, samples):
    running = None
    for tap_index in range(9):
        neighbour = lax.slice_in_dim(padded, tap_index, tap_index + count, axis=axis)
        moved = jnp.zeros(neighbour.shape[:-1] + (samples,), jnp.float32)
        for dip_value in range(-dip_limit, dip_limit + 1):
            first_sample = time_pad + (tap_index - 4) * dip_value
            moved = jnp.where(
                (dips == dip_value)[..., None],
                neighbour[..., first_sample : first_sample + samples],
                moved,
            )
        term = FILTER_TAPS[tap_index] * moved
        running = term if running is None else running + term
    return running


def any_load(traces, destination, bin_local, offset_class, dip_inline, dip_xline):
    n_inline = lax.axis_size("inline")
    n_xline = lax.axis_size("xline")
    devices = n_inline * n_xline
    row_count, samples = traces.shape
    capacity = 3 * row_count // devices
    inline_bins, xline_bins = dip_inline.shape
    bin_count = inline_bins * xline_bins
    target = destination[:, 0]
    matches = (target[:, None] == jnp.arange(devices, dtype=jnp.int32)[None, :]).astype(jnp.int32)
    before = jnp.cumsum(matches, axis=0) - matches
    position = jnp.sum(before * matches, axis=1)
    slot_index = target * capacity + position
    labels = offset_class * bin_count + bin_local
    outgoing = jnp.zeros((devices * capacity, samples), jnp.bfloat16).at[slot_index].set(traces)
    outgoing = outgoing.reshape(n_inline, n_xline, capacity, samples)
    out_labels = jnp.full((devices * capacity,), -1, jnp.int32).at[slot_index].set(labels)
    out_labels = out_labels.reshape(n_inline, n_xline, capacity)

    def exchange(value):
        value = lax.all_to_all(value, "inline", split_axis=0, concat_axis=0, tiled=True)
        return lax.all_to_all(value, "xline", split_axis=1, concat_axis=1, tiled=True)

    received = exchange(outgoing).reshape(-1, samples)
    got_labels = exchange(out_labels).reshape(-1)
    cell_total = OFFSETS * bin_count
    selector = jnp.arange(cell_total, dtype=jnp.int32)[:, None] == got_labels[None, :]
    totals = jnp.dot(selector.astype(jnp.bfloat16), received, preferred_element_type=jnp.float32)
    counts = jnp.sum(selector.astype(jnp.int32), axis=1).astype(jnp.float32)
    stacked = (totals / jnp.maximum(counts, 1.0)[:, None]).reshape(
        OFFSETS, inline_bins, xline_bins, samples
    )
    with_rim = padded_2(stacked, (("inline", 1),), 4)
    padded = jnp.pad(with_rim, ((0, 0), (0, 0), (0, 0), (time_pad, time_pad)))
    smoothed = dip_pass(padded, dip_inline, 1, inline_bins, samples)
    with_rim = padded_2(smoothed, (("xline", 2),), 4)
    padded = jnp.pad(with_rim, ((0, 0), (0, 0), (0, 0), (time_pad, time_pad)))
    return dip_pass(padded, dip_xline, 2, xline_bins, samples)


def per_device(traces, destination, bin_local, offset_class, dip_inline, dip_xline):
    n = traces.shape[0]
    first, flag = route(
        dip_inline,
        traces,
        destination.reshape(1, n),
        bin_local.reshape(1, n),
        offset_class.reshape(1, n),
    )
    return lax.cond(
        flag[0, 0] > 0,
        lambda: any_load(traces, destination, bin_local, offset_class, dip_inline, dip_xline),
        lambda: xline_pass(dip_xline, first),
    )


def solution(mesh):
    return jax.shard_map(
        per_device,
        mesh=mesh,
        in_specs=(
            P(("inline", "xline"), None),
            P(("inline", "xline"), None),
            P(("inline", "xline")),
            P(("inline", "xline")),
            P("inline", "xline"),
            P("inline", "xline"),
        ),
        out_specs=P(None, "inline", "xline", None),
        check_vma=False,
    )
```

```python
import jax
import jax.numpy as jnp
from jax import lax
from jax.experimental import pallas as pl
from jax.experimental.pallas import tpu as pltpu
from jax.sharding import PartitionSpec as P

OFFSETS = 8
FILTER_TAPS = (0.05, 0.08, 0.12, 0.15, 0.2, 0.15, 0.12, 0.08, 0.05)
dip_limit = 3
time_pad = 12

MESH = pl.DeviceIdType.MESH
N_Z = 8
N_P = 32
N_XL = 8
N_IL = 32
CAP = 6
POOL = 96
SLOTS = N_Z * CAP
ROWS = N_P * SLOTS
CELLS = 512
BINS = CELLS // OFFSETS
WIDTHS = (128, 256, 256, 256, 128)
STARTS = (0, 128, 384, 640, 896)
T = len(WIDTHS)
W = max(WIDTHS)
UNROLL = 4
NT = (((1,), (1,)), ((), ()))
f32, bf16, i32 = jnp.float32, jnp.bfloat16, jnp.int32


def iota(shape, dim):
    return lax.broadcasted_iota(i32, shape, dim)


def onehot(mask):
    return jnp.where(mask, 1.0, 0.0).astype(bf16)


def steer(at, dip, parts, ks):
    lane = iota((OFFSETS, 128), 1)
    zero = jnp.zeros((OFFSETS, 128), f32)

    def piece(j, k):
        if not 0 <= k < parts:
            return zero
        ref, index = at(j)
        return ref[index + (slice(None), slice(k * 128, (k + 1) * 128))]

    def moved(j):
        shift = j * dip
        after = lane < shift
        before = lane >= 128 + shift
        turn = lax.rem(128 - shift, 128)
        row = [piece(j, k) for k in range(ks[0] - 1, ks[-1] + 2)]
        return [
            pltpu.roll(jnp.where(after, row[i + 2], jnp.where(before, row[i], row[i + 1])), turn, 1)
            for i in range(len(ks))
        ]

    acc = [FILTER_TAPS[4] * piece(0, k) for k in ks]
    for j in (1, 2, 3, 4):
        up, down = moved(j), moved(-j)
        acc = [a + FILTER_TAPS[4 + j] * (u + v) for a, u, v in zip(acc, up, down)]
    return acc


def route_kernel(
    dips, traces_hbm, dest, bins, offs, out_hbm, flag_out,
    traces, out, ext, rows, eye, p1, send1, recv1, lab1s, lab1r, l2, p2, send2, recv2, lab2s, lab2r, wide, sel, share,
    rim_q, rim_s, got_q, got_s, relay, edge, got_e,
    s1_send, s1_recv, l1_send, l1_recv, s2_send, s2_recv, l2_send, l2_recv,
    q_send, q_recv, f_send, f_recv, e_send, e_recv, r_send, r_recv, in_sem, out_sem,
):
    n, samples = traces.shape
    parts = samples // 128

    def span(t):
        return slice(STARTS[t], STARTS[t] + WIDTHS[t])

    def wide_of(t):
        return pl.ds(0, WIDTHS[t])

    me_i = lax.axis_index("inline")
    me_x = lax.axis_index("xline")
    my_z = lax.rem(me_i, N_Z)
    my_col = me_i // N_Z
    my_p = my_col * N_XL + me_x

    def fetch(t):
        return pltpu.make_async_copy(
            traces_hbm.at[:, pl.ds(STARTS[t], WIDTHS[t])], traces.at[:, pl.ds(STARTS[t], WIDTHS[t])], in_sem.at[t]
        )

    def give(t):
        lanes = pl.ds(STARTS[t], WIDTHS[t])
        return pltpu.make_async_copy(out.at[:, :, :, lanes], out_hbm.at[:, :, :, lanes], out_sem.at[t])

    for t in range(T):
        fetch(t).start()

    def z_peer(k):
        z = lax.rem(my_z + k, N_Z)
        return z, (my_col * N_Z + z, me_x)

    def p_peer(k):
        p = lax.rem(my_p + k, N_P)
        return p, ((p // N_XL) * N_Z + my_z, lax.rem(p, N_XL))

    def rim_peer(side):
        return (lax.rem(me_i + (1 if side == 0 else N_IL - 1), N_IL), me_x)

    barrier = pltpu.get_barrier_semaphore()
    for side in range(2):
        pl.semaphore_signal(barrier, inc=1, device_id=rim_peer(side), device_id_type=MESH)

    @pl.loop(1, N_Z)
    def _(k):
        pl.semaphore_signal(barrier, inc=1, device_id=z_peer(k)[1], device_id_type=MESH)

    @pl.loop(1, N_P, unroll=4)
    def _(k):
        pl.semaphore_signal(barrier, inc=1, device_id=p_peer(k)[1], device_id_type=MESH)

    d = dest[...]
    eye[...] = onehot(iota((n, n), 0) == iota((n, n), 1))
    wide_d = jnp.broadcast_to(d.astype(f32), (128, n)).astype(bf16)
    dcol = lax.dot_general(eye[...], wide_d, NT, preferred_element_type=f32).astype(i32)
    zcol = (dcol >> 3) & 7
    for t in range(n // 128):
        lanes = slice(t * 128, (t + 1) * 128)
        drow = d[:, lanes]
        earlier = iota((n, 128), 0) < iota((n, 128), 1) + t * 128
        same = (dcol == drow) & earlier
        same_z = (zcol == ((drow >> 3) & 7)) & earlier
        rows[0:1, lanes] = jnp.sum(jnp.where(same, 1.0, 0.0), axis=0, keepdims=True)
        rows[1:2, lanes] = jnp.sum(jnp.where(same_z, 1.0, 0.0), axis=0, keepdims=True)
    position = rows[0:1, :].astype(i32)
    place = rows[1:2, :].astype(i32)
    zrow = (d >> 3) & 7
    plane = (d >> 6) * N_XL + (d & 7)
    over = jnp.max(place, axis=1, keepdims=True) >= POOL
    over = jnp.where(over, 1, 0)
    sub = iota((16, n), 0)
    labels = jnp.where(sub == 0, plane, 0)
    labels = jnp.where(sub == 1, my_z * CAP + position + 1, labels)
    labels = jnp.where(sub == 2, bins[...], labels)
    labels = jnp.where(sub == 3, offs[...], labels)
    labels = labels.astype(f32).astype(bf16)

    @pl.loop(0, N_Z)
    def _(z):
        target = jnp.where(zrow == z, place, -1)
        pick = onehot(iota((128, n), 0) == target)
        p1[z] = pick[:POOL]
        lab = lax.dot_general(labels, pick, NT, preferred_element_type=f32)[:8].astype(i32)
        lab = jnp.where(iota((8, 128), 1) < POOL, lab, 0)
        lab1s[z] = jnp.where(iota((8, 128), 0) == 4, over, lab)

    lab1r[my_z] = lab1s[my_z]

    pl.semaphore_wait(barrier, N_Z - 1 + N_P - 1 + 2)

    def lab1_copy(k):
        z, peer = z_peer(k)
        return pltpu.make_async_remote_copy(
            src_ref=lab1s.at[z], dst_ref=lab1r.at[my_z],
            send_sem=l1_send.at[0], recv_sem=l1_recv.at[0],
            device_id=peer, device_id_type=MESH,
        )

    def row1_copy(t, k):
        z, peer = z_peer(k)
        return pltpu.make_async_remote_copy(
            src_ref=send1.at[t, z, :, wide_of(t)], dst_ref=recv1.at[t, my_z, :, wide_of(t)],
            send_sem=s1_send.at[t], recv_sem=s1_recv.at[t],
            device_id=peer, device_id_type=MESH,
        )

    def lab2_copy(k):
        p, peer = p_peer(k)
        return pltpu.make_async_remote_copy(
            src_ref=lab2s.at[p], dst_ref=lab2r.at[my_p],
            send_sem=l2_send.at[0], recv_sem=l2_recv.at[0],
            device_id=peer, device_id_type=MESH,
        )

    def row2_copy(t, k):
        p, peer = p_peer(k)
        return pltpu.make_async_remote_copy(
            src_ref=send2.at[t, p, :, wide_of(t)], dst_ref=recv2.at[t, my_p, :, wide_of(t)],
            send_sem=s2_send.at[t], recv_sem=s2_recv.at[t],
            device_id=peer, device_id_type=MESH,
        )

    def all_of(src, dst, send, recv, peer):
        return pltpu.make_async_remote_copy(
            src_ref=src, dst_ref=dst, send_sem=send, recv_sem=recv, device_id=peer, device_id_type=MESH
        )

    z_others, p_others = pl.ds(0, N_Z - 1), pl.ds(0, N_P - 1)
    lab1_all = all_of(lab1s.at[z_others], lab1r.at[z_others], l1_send.at[0], l1_recv.at[0], z_peer(1)[1])
    lab2_all = all_of(lab2s.at[p_others], lab2r.at[p_others], l2_send.at[0], l2_recv.at[0], p_peer(1)[1])

    def row1_all(t):
        return all_of(
            send1.at[t, z_others, :, wide_of(t)], recv1.at[t, z_others, :, wide_of(t)],
            s1_send.at[t], s1_recv.at[t], z_peer(1)[1],
        )

    def row2_all(t):
        return all_of(
            send2.at[t, p_others, :, wide_of(t)], recv2.at[t, p_others, :, wide_of(t)],
            s2_send.at[t], s2_recv.at[t], p_peer(1)[1],
        )

    @pl.loop(1, N_Z)
    def _(k):
        lab1_copy(k).start()

    def send_rows(t):
        fetch(t).wait()
        picked = jnp.dot(
            p1[...].reshape(N_Z * POOL, n), traces[:, span(t)], preferred_element_type=f32
        )
        send1[t, :, :, wide_of(t)] = picked.astype(bf16).reshape(N_Z, POOL, WIDTHS[t])

        @pl.loop(1, N_Z, unroll=7)
        def _(k):
            row1_copy(t, k).start()

        recv1[t, my_z, :, wide_of(t)] = send1[t, my_z, :, wide_of(t)]

    send_rows(0)
    send_rows(1)

    lab1_all.wait_recv()

    lab = jnp.concatenate([lab1r[z][:, :POOL] for z in range(N_Z)], axis=1)
    code = lab[1:2, :]
    wide[:, 0:N_Z * POOL] = jnp.where(code > 0, lab[0:1, :] * SLOTS + code - 1, -1) + jnp.zeros_like(lab)
    l2[...] = jnp.concatenate([lab, lab], axis=0).astype(f32).astype(bf16)
    worst = jnp.max(lab[4:5, :], axis=1, keepdims=True)

    @pl.loop(0, N_Z * POOL // 128)
    def _(c):
        lanes = pl.ds(pl.multiple_of(c * 128, 128), 128)
        p2[:, lanes] = onehot(iota((ROWS, 128), 0) == wide[0:1, lanes])

    lab = lax.dot_general(l2[...], p2[...], NT, preferred_element_type=f32).astype(i32)
    cell = jnp.where(lab[1:2, :] > 0, lab[2:3, :] * OFFSETS + lab[3:4, :], -1)
    wide[...] = jnp.where(iota((8, ROWS), 0) == 1, worst, cell)

    @pl.loop(0, N_P // 8)
    def _(g):
        part = wide[:, pl.ds(pl.multiple_of(g * 8 * SLOTS, 128), 8 * SLOTS)]
        for i in range(8):
            lab2s[g * 8 + i, :, 0:SLOTS] = part[:, i * SLOTS:(i + 1) * SLOTS]

    lab2r[my_p] = lab2s[my_p]

    @pl.loop(1, N_P)
    def _(k):
        lab2_copy(k).start()

    def forward(t):
        row1_all(t).wait_recv()

        if t + 2 < T:
            send_rows(t + 2)
        arrived = recv1[t, :, :, wide_of(t)].reshape(N_Z * POOL, WIDTHS[t])
        half = ROWS // 2
        for g in range(2):
            moved = jnp.dot(p2[g * half:(g + 1) * half, :], arrived, preferred_element_type=f32)
            moved = moved.astype(bf16).reshape(N_P // 2, SLOTS, WIDTHS[t])
            send2[t, g * (N_P // 2):(g + 1) * (N_P // 2), :, wide_of(t)] = moved

        @pl.loop(1, N_P, unroll=4)
        def _(k):
            row2_copy(t, k).start()

        recv2[t, my_p, :, wide_of(t)] = send2[t, my_p, :, wide_of(t)]

    def selector():
        lab2_all.wait_recv()
        lab1_all.wait_send()

        @pl.loop(0, N_P // 8)
        def _(g):
            part = jnp.concatenate([lab2r[g * 8 + i][:, 0:SLOTS] for i in range(8)], axis=1)
            wide[:, pl.ds(pl.multiple_of(g * 8 * SLOTS, 128), 8 * SLOTS)] = part

        @pl.loop(0, ROWS // 128)
        def _(c):
            lanes = pl.ds(pl.multiple_of(c * 128, 128), 128)
            sel[:, lanes] = onehot(iota((CELLS, 128), 0) == wide[0:1, lanes])

        per_cell = jnp.dot(sel[...], jnp.ones((ROWS, 128), bf16), preferred_element_type=f32)
        share[...] = 1.0 / jnp.maximum(per_cell, 1.0)
        flag_out[...] = jnp.broadcast_to(jnp.max(wide[1:2, :], axis=1, keepdims=True), (8, 128))

    def stack(t):
        row2_all(t).wait_recv()

        total = jnp.dot(sel[...], recv2[t, :, :, wide_of(t)].reshape(ROWS, WIDTHS[t]), preferred_element_type=f32)
        parts = [total[:, c * 128:(c + 1) * 128] * share[...] for c in range(WIDTHS[t] // 128)]
        top = jnp.abs(parts[0])
        for c, part in enumerate(parts):
            lanes = slice(STARTS[t] + c * 128, STARTS[t] + (c + 1) * 128)
            ext[BINS:2 * BINS, :, lanes] = part.reshape(BINS, OFFSETS, 128)
            top = jnp.maximum(top, jnp.abs(part))
        step = (jnp.max(top, axis=1, keepdims=True) * (1.01 / 32767.0)).astype(bf16)
        step = jnp.broadcast_to(step, (CELLS, 128))
        size = step.astype(f32)
        fine = jnp.where(size > 0.0, 1.0 / size, 0.0)
        for c, part in enumerate(parts):
            rim_q[t, :, c * 128:(c + 1) * 128] = jnp.round(part * fine).astype(i32).astype(jnp.int16)
        first_lane = onehot(iota((16, 128), 1) == 0)
        rim_s[t] = lax.dot_general(first_lane, step, NT, preferred_element_type=f32)[:8]
        send_rim(t)

    def size_copy(t, side):
        return pltpu.make_async_remote_copy(
            src_ref=rim_s.at[t], dst_ref=got_s.at[side, t],
            send_sem=f_send.at[side, t], recv_sem=f_recv.at[side, t],
            device_id=rim_peer(side), device_id_type=MESH,
        )

    def rim_copy(t, side, h):
        return pltpu.make_async_remote_copy(
            src_ref=rim_q.at[t, rim_half(h), wide_of(t)], dst_ref=got_q.at[side, t, rim_half(h), wide_of(t)],
            send_sem=q_send.at[side, t, h], recv_sem=q_recv.at[side, t, h],
            device_id=rim_peer(side), device_id_type=MESH,
        )

    def relay_copy(t, side):
        return pltpu.make_async_remote_copy(
            src_ref=rim_q.at[t, rim_half(1), wide_of(t)], dst_ref=relay.at[t, :, wide_of(t)],
            send_sem=q_send.at[side, t, 1], recv_sem=r_recv.at[t],
            device_id=(lax.rem(me_i + (N_Z if side == 0 else N_IL - N_Z), N_IL), me_x), device_id_type=MESH,
        )

    def onward_copy(t, side):
        return pltpu.make_async_remote_copy(
            src_ref=relay.at[t, :, wide_of(t)], dst_ref=got_q.at[side, t, rim_half(1), wide_of(t)],
            send_sem=r_send.at[t], recv_sem=q_recv.at[side, t, 1],
            device_id=(my_col * N_Z + (0 if side == 0 else N_Z - 1), me_x), device_id_type=MESH,
        )

    def rim_half(h):
        return pl.ds(h * CELLS // 2, CELLS // 2)

    def last_plane(side):
        return my_z == (N_Z - 1 if side == 0 else 0)

    def send_rim(t):
        for side in range(2):
            size_copy(t, side).start()
            rim_copy(t, side, 0).start()

            @pl.when(last_plane(side))
            def _():
                relay_copy(t, side).start()

            @pl.when(jnp.logical_not(last_plane(side)))
            def _():
                rim_copy(t, side, 1).start()

    def pass_on(t):
        for side in range(2):
            @pl.when(last_plane(side))
            def _():
                relay_copy(t, side).wait_recv()
                onward_copy(t, side).start()

    def wait_rim(t, side):
        size_copy(t, side).wait_recv()
        rim_copy(t, side, 0).wait_recv()
        rim_copy(t, side, 1).wait_recv()

    def sent(t):
        row1_all(t).wait_send()
        row2_all(t).wait_send()
        for side in range(2):
            size_copy(t, side).wait_send()
            rim_copy(t, side, 0).wait_send()
            rim_copy(t, side, 1).wait_send()

            @pl.when(last_plane(side))
            def _():
                onward_copy(t, side).wait_send()

    def rim(t, side):
        wait_rim(t, side)
        row = jnp.broadcast_to(got_s[side, t][0:1, :], (128, CELLS)).astype(bf16)
        size = lax.dot_general(eye[...], row, NT, preferred_element_type=f32)
        outside = me_i == (0 if side == 0 else N_IL - 1)
        size = size * jnp.where(outside, 0.0, 1.0)
        base = 0 if side == 0 else 2 * BINS
        for c in range(WIDTHS[t] // 128):
            value = got_q[side, t, :, c * 128:(c + 1) * 128].astype(f32)
            lanes = slice(STARTS[t] + c * 128, STARTS[t] + (c + 1) * 128)
            ext[base:base + BINS, :, lanes] = (value * size).reshape(BINS, OFFSETS, 128)

    n_il, n_xl = dips.shape

    def edge_copy(t, side):
        x = lax.rem(me_x + (1 if side == 0 else N_XL - 1), N_XL)
        return pltpu.make_async_remote_copy(
            src_ref=edge.at[side, t, :, :, :, wide_of(t)], dst_ref=got_e.at[side, t, :, :, :, wide_of(t)],
            send_sem=e_send.at[side, t], recv_sem=e_recv.at[side, t],
            device_id=(me_i, x), device_id_type=MESH,
        )

    def inline_pass(t):
        ks = range(STARTS[t] // 128, (STARTS[t] + WIDTHS[t]) // 128)

        def column(x):
            for i in range(n_il):
                acc = steer(lambda j, i=i: (ext, ((i + 4 + j) * n_xl + x,)), dips[i, x], parts, ks)
                for k, part in zip(ks, acc):
                    out[i, x + 4, :, k * 128:(k + 1) * 128] = part

        pl.loop(0, 4, unroll=UNROLL)(column)
        pl.loop(n_xl - 4, n_xl, unroll=UNROLL)(column)
        edge[0, t, :, :, :, wide_of(t)] = out[:, n_xl:n_xl + 4, :, span(t)]
        edge[1, t, :, :, :, wide_of(t)] = out[:, 4:8, :, span(t)]
        for side in range(2):
            edge_copy(t, side).start()
        pl.loop(4, n_xl - 4, unroll=UNROLL)(column)

    def edges(t):
        lanes = span(t)
        for side in range(2):
            edge_copy(t, side).wait()
            outside = me_x == (0 if side == 0 else N_XL - 1)
            value = got_e[side, t, :, :, :, wide_of(t)] * jnp.where(outside, 0.0, 1.0)
            if side == 0:
                out[:, 0:4, :, lanes] = value
            else:
                out[:, n_xl + 4:, :, lanes] = value
        give(t).start()
        sent(t)

    def rims(t):
        for side in range(2):
            rim(t, side)

    for t in range(T + 5):
        if t < T:
            forward(t)
        if t == 0:
            selector()
        if 0 <= t - 2 < T:
            pass_on(t - 2)
        if 0 <= t - 1 < T:
            stack(t - 1)
        if 0 <= t - 3 < T:
            rims(t - 3)
        if 0 <= t - 4 < T:
            inline_pass(t - 4)
        if 0 <= t - 5 < T:
            edges(t - 5)
    lab2_all.wait_send()
    for t in range(T):
        give(t).wait()


def route(dips, traces, dest, bins, offs):
    n, samples = traces.shape
    n_il, n_xl = dips.shape
    w = W
    hbm = pl.BlockSpec(memory_space=pltpu.HBM)
    vmem = pl.BlockSpec(memory_space=pltpu.VMEM)
    dma = pltpu.SemaphoreType.DMA
    return pl.pallas_call(
        route_kernel,
        out_shape=(
            jax.ShapeDtypeStruct((n_il, n_xl + 8, OFFSETS, samples), f32),
            jax.ShapeDtypeStruct((8, 128), i32),
        ),
        in_specs=[pl.BlockSpec(memory_space=pltpu.SMEM), hbm] + [vmem] * 3,
        out_specs=(hbm, vmem),
        scratch_shapes=[
            pltpu.VMEM((n, samples), bf16),
            pltpu.VMEM((n_il, n_xl + 8, OFFSETS, samples), f32),
            pltpu.VMEM((3 * BINS, OFFSETS, samples), f32),
            pltpu.VMEM((8, n), f32),
            pltpu.VMEM((n, n), bf16),
            pltpu.VMEM((N_Z, POOL, n), bf16),
            pltpu.VMEM((T, N_Z, POOL, w), bf16),
            pltpu.VMEM((T, N_Z, POOL, w), bf16),
            pltpu.VMEM((N_Z, 8, 128), i32),
            pltpu.VMEM((N_Z, 8, 128), i32),
            pltpu.VMEM((16, N_Z * POOL), bf16),
            pltpu.VMEM((ROWS, N_Z * POOL), bf16),
            pltpu.VMEM((T, N_P, SLOTS, w), bf16),
            pltpu.VMEM((T, N_P, SLOTS, w), bf16),
            pltpu.VMEM((N_P, 8, 128), i32),
            pltpu.VMEM((N_P, 8, 128), i32),
            pltpu.VMEM((8, ROWS), i32),
            pltpu.VMEM((CELLS, ROWS), bf16),
            pltpu.VMEM((CELLS, 128), f32),
            pltpu.VMEM((T, CELLS, w), jnp.int16),
            pltpu.VMEM((T, 8, CELLS), f32),
            pltpu.VMEM((2, T, CELLS, w), jnp.int16),
            pltpu.VMEM((2, T, 8, CELLS), f32),
            pltpu.VMEM((T, CELLS // 2, w), jnp.int16),
            pltpu.VMEM((2, T, n_il, 4, OFFSETS, w), f32),
            pltpu.VMEM((2, T, n_il, 4, OFFSETS, w), f32),
            dma((T,)), dma((T,)), dma((1,)), dma((1,)),
            dma((T,)), dma((T,)), dma((1,)), dma((1,)),
            dma((2, T, 2)), dma((2, T, 2)), dma((2, T)), dma((2, T)), dma((2, T)), dma((2, T)),
            dma((T,)), dma((T,)), dma((T,)), dma((T,)),
        ],
        compiler_params=pltpu.CompilerParams(
            collective_id=0, has_side_effects=True, vmem_limit_bytes=48 * 1024 * 1024
        ),
    )(dips, traces, dest, bins, offs)


def xline_kernel(dips, ext, out, turned):
    n_xl, samples = out.shape[2], out.shape[3]
    il = pl.program_id(0)
    first = pl.program_id(1) * n_xl
    ks = range(samples // 128)

    def column(x, carry):
        acc = steer(lambda j: (ext, (0, first + x + 4 + j)), dips[il, first + x], len(ks), ks)
        for k, part in zip(ks, acc):
            turned[k, pl.ds(x, OFFSETS, stride=n_xl), :] = part
        return carry

    lax.fori_loop(0, n_xl, column, 0, unroll=16)
    for k in ks:
        out[:, 0, :, k * 128:(k + 1) * 128] = turned[k].reshape(OFFSETS, n_xl, 128)


def xline_pass(dips, ext):
    n_il, n_xl = dips.shape
    samples = ext.shape[-1]
    step = n_xl
    return pl.pallas_call(
        xline_kernel,
        grid=(n_il, n_xl // step),
        out_shape=jax.ShapeDtypeStruct((OFFSETS, n_il, n_xl, samples), f32),
        in_specs=[
            pl.BlockSpec(memory_space=pltpu.SMEM),
            pl.BlockSpec((1, n_xl + 8, OFFSETS, samples), lambda s, h: (s, 0, 0, 0)),
        ],
        out_specs=pl.BlockSpec((OFFSETS, 1, step, samples), lambda s, h: (0, s, h, 0)),
        scratch_shapes=[pltpu.VMEM((samples // 128, OFFSETS * step, 128), f32)],
        compiler_params=pltpu.CompilerParams(vmem_limit_bytes=60 * 1024 * 1024),
    )(dips, ext)


def padded_2(cells, sides, width):
    for axis, dim in sides:
        count = lax.axis_size(axis)
        ends = count - 1
        head = lax.slice_in_dim(cells, 0, width, axis=dim)
        tail = lax.slice_in_dim(cells, cells.shape[dim] - width, cells.shape[dim], axis=dim)
        cells = jnp.concatenate(
            [
                lax.ppermute(tail, axis, [(i, (i + 1) % count) for i in range(ends)]),
                cells,
                lax.ppermute(head, axis, [((i + 1) % count, i) for i in range(ends)]),
            ],
            axis=dim,
        )
    return cells


def dip_pass(padded, dips, axis, count, samples):
    running = None
    for tap_index in range(9):
        neighbour = lax.slice_in_dim(padded, tap_index, tap_index + count, axis=axis)
        moved = jnp.zeros(neighbour.shape[:-1] + (samples,), jnp.float32)
        for dip_value in range(-dip_limit, dip_limit + 1):
            first_sample = time_pad + (tap_index - 4) * dip_value
            moved = jnp.where(
                (dips == dip_value)[..., None],
                neighbour[..., first_sample : first_sample + samples],
                moved,
            )
        term = FILTER_TAPS[tap_index] * moved
        running = term if running is None else running + term
    return running


def any_load(traces, destination, bin_local, offset_class, dip_inline, dip_xline):
    n_inline = lax.axis_size("inline")
    n_xline = lax.axis_size("xline")
    devices = n_inline * n_xline
    row_count, samples = traces.shape
    capacity = 3 * row_count // devices
    inline_bins, xline_bins = dip_inline.shape
    bin_count = inline_bins * xline_bins
    target = destination[:, 0]
    matches = (target[:, None] == jnp.arange(devices, dtype=jnp.int32)[None, :]).astype(jnp.int32)
    before = jnp.cumsum(matches, axis=0) - matches
    position = jnp.sum(before * matches, axis=1)
    slot_index = target * capacity + position
    labels = offset_class * bin_count + bin_local
    outgoing = jnp.zeros((devices * capacity, samples), jnp.bfloat16).at[slot_index].set(traces)
    outgoing = outgoing.reshape(n_inline, n_xline, capacity, samples)
    out_labels = jnp.full((devices * capacity,), -1, jnp.int32).at[slot_index].set(labels)
    out_labels = out_labels.reshape(n_inline, n_xline, capacity)

    def exchange(value):
        value = lax.all_to_all(value, "inline", split_axis=0, concat_axis=0, tiled=True)
        return lax.all_to_all(value, "xline", split_axis=1, concat_axis=1, tiled=True)

    received = exchange(outgoing).reshape(-1, samples)
    got_labels = exchange(out_labels).reshape(-1)
    cell_total = OFFSETS * bin_count
    selector = jnp.arange(cell_total, dtype=jnp.int32)[:, None] == got_labels[None, :]
    totals = jnp.dot(selector.astype(jnp.bfloat16), received, preferred_element_type=jnp.float32)
    counts = jnp.sum(selector.astype(jnp.int32), axis=1).astype(jnp.float32)
    stacked = (totals / jnp.maximum(counts, 1.0)[:, None]).reshape(
        OFFSETS, inline_bins, xline_bins, samples
    )
    with_rim = padded_2(stacked, (("inline", 1),), 4)
    padded = jnp.pad(with_rim, ((0, 0), (0, 0), (0, 0), (time_pad, time_pad)))
    smoothed = dip_pass(padded, dip_inline, 1, inline_bins, samples)
    with_rim = padded_2(smoothed, (("xline", 2),), 4)
    padded = jnp.pad(with_rim, ((0, 0), (0, 0), (0, 0), (time_pad, time_pad)))
    return dip_pass(padded, dip_xline, 2, xline_bins, samples)


def per_device(traces, destination, bin_local, offset_class, dip_inline, dip_xline):
    n = traces.shape[0]
    first, flag = route(
        dip_inline,
        traces,
        destination.reshape(1, n),
        bin_local.reshape(1, n),
        offset_class.reshape(1, n),
    )
    return lax.cond(
        flag[0, 0] > 0,
        lambda: any_load(traces, destination, bin_local, offset_class, dip_inline, dip_xline),
        lambda: xline_pass(dip_xline, first),
    )


def solution(mesh):
    return jax.shard_map(
        per_device,
        mesh=mesh,
        in_specs=(
            P(("inline", "xline"), None),
            P(("inline", "xline"), None),
            P(("inline", "xline")),
            P(("inline", "xline")),
            P("inline", "xline"),
            P("inline", "xline"),
        ),
        out_specs=P(None, "inline", "xline", None),
        check_vma=False,
    )
```
